32 devices in a mesh: grp: 4 (over z), blk: 8 (over y, x, core).
Axes of the slice: x: 2, y: 2, z: 4, core: 2. Of those that a mesh axis runs over, the one named last changes fastest.
Arguments:
- state: float32 [8, 8, 8, 8, 16384], P(None, None, None, None, ('grp', 'blk')), may hold values from -6 to 6
- counts: int32 [32], P(('grp', 'blk')), may hold values from 384 to 512, as said below
- neighbours: int32 [6, 16384], P(None, ('grp', 'blk')), may hold values from -1 to 16383, as said below
- rows: int32 [16384], P(('grp', 'blk')), may hold values from -1 to 24575, as said below
- rates: float32 [8], replicated, may hold values from 0.02 to 0.16
- conductance: float32 [96, 256], P('blk'), may hold values from 0.5 to 4
Outputs:
- new_state: float32 [8, 8, 8, 8, 16384], P(None, None, None, None, ('grp', 'blk'))
- potential: float32 [96, 256], P('blk')
The draws below stay inside these ranges and needn't reach their ends.
Inputs may be any that keep to these rules, and one draw needn't show every extreme that they name: `counts`: device 0 has exactly 512 live blocks; live blocks are the first ones of a device's slots. `neighbours`: padded slots name -1 on every face. A live block of device d names a live block of d itself, of d - 1 among its last 128 live blocks, of d + 1 among its first 128 blocks, or -1. `rows`: padded slots have -1; several blocks may name one cell.
All inputs are finite; a program needn't handle non-finite values.
Results may differ from the reference program's by a relative error of at most 0.0001.
Values sent between devices are 32-bit elements; how exact they have to be, the bound alone decides.
A program may use at most 256 MiB of HBM per device.

```python
import math
import jax
import jax.numpy as jnp

VARS = 8
BS = 8
NB = 512
STEPS = 2
ITERS = 3
NLON = 256
EDGE = 128
BLOCKS = 16384
NLAT = 96
NI = 24576
DEVICES = 32


def block_counts(key):
    drawn = jax.random.randint(jax.random.fold_in(key, 11), (DEVICES,), NB - NB // 4, NB + 1)
    return drawn.at[0].set(NB).astype(jnp.int32)


def draw_counts(key, part):
    return block_counts(key)


def draw_neighbours(key, part):
    totals = block_counts(key)
    key = jax.random.fold_in(key, 5)
    slots = jnp.arange(BLOCKS, dtype=jnp.int32)
    device = slots // NB
    local = slots % NB
    count_here = totals[device]
    count_below = totals[jnp.maximum(device - 1, 0)]
    alive = local < count_here
    first_key, second_key = jax.random.split(key)
    category = jax.random.randint(first_key, (6, BLOCKS), 0, 20)
    picks = jax.random.randint(second_key, (6, BLOCKS), 0, 1 << 20)
    inside = device * NB + picks % count_here
    lower = jnp.where(device > 0, (device - 1) * NB + count_below - EDGE + picks % EDGE, -1)
    upper = jnp.where(device < DEVICES - 1, (device + 1) * NB + picks % EDGE, -1)
    faces = jnp.arange(6, dtype=jnp.int32)[:, None]
    remote = jnp.where(faces % 2 == 0, lower, upper)
    chosen = jnp.where(category < 3, -1, jnp.where(category < 7, remote, inside))
    forced_low = jnp.where(device > 0, (device - 1) * NB + count_below - EDGE, -1)
    forced_high = jnp.where(device < DEVICES - 1, (device + 1) * NB + EDGE - 1, -1)
    chosen = chosen.at[0].set(jnp.where(local == 0, forced_low, chosen[0]))
    chosen = chosen.at[1].set(jnp.where(local == 0, forced_high, chosen[1]))
    return jnp.where(alive[None, :], chosen, -1).astype(jnp.int32)


def draw_rows(key, part):
    totals = block_counts(key)
    key = jax.random.fold_in(key, 7)
    slots = jnp.arange(BLOCKS, dtype=jnp.int32)
    device = slots // NB
    alive = slots % NB < totals[device]
    first_key, second_key = jax.random.split(key)
    inner = jax.random.randint(first_key, (BLOCKS,), 0, 8) < device % 4 + 1
    target = jax.random.randint(second_key, (BLOCKS,), 0, NI)
    chosen = jnp.where(inner & alive, target, -1)
    return chosen.at[0].set(NI - 1).astype(jnp.int32)


def level_of(own_key, shape, shards, smallest, largest):
    level, own = 1.0, jax.random.fold_in(own_key, 6)
    for position, parts in shards:
        steps = jnp.exp(jax.random.uniform(jax.random.fold_in(own, position), (parts,), jnp.float32, smallest / len(shards), largest / len(shards)))
        level = level * jnp.repeat(steps, shape[position] // parts).reshape([-1 if axis == position else 1 for axis in range(len(shape))])
    return level


def bell_draw(key, shape, width, limit, pieces=(), kind=jnp.bfloat16):
    factor_of = level_of(key, shape, pieces, -0.22, 0.18) if pieces else 1.0
    values = jax.random.normal(key, shape, jnp.float32) * width * factor_of
    return jnp.minimum(jnp.maximum(values, -limit), limit).astype(kind)


def setup_inputs(seed: int = 0) -> dict:
    splits = jax.random.split(jax.random.key(seed), 7)
    return {
        "state": bell_draw(splits[0], (VARS, BS, BS, BS, BLOCKS), 1.0, 6.0, ((4, 32),), jnp.float32),
        "counts": draw_counts(jax.random.fold_in(splits[6], 71), 0),
        "neighbours": draw_neighbours(jax.random.fold_in(splits[6], 71), 0),
        "rows": draw_rows(jax.random.fold_in(splits[6], 71), 0),
        "rates": jnp.clip(jnp.exp(jax.random.uniform(splits[4], (VARS,), jnp.float32, math.log(0.02), math.log(0.16))), 0.02, 0.16),
        "conductance": jnp.clip(jnp.exp(math.log(4.0) - 2.0794415 * jax.random.uniform(splits[5], (NLAT, NLON), jnp.float32) ** level_of(splits[5], (NLAT, NLON), ((0, 8),), -0.2, 0.2)), 0.5, 4.0),
    }


def planes(u):
    return jnp.stack([u[:, 0], u[:, -1], u[:, :, 0], u[:, :, -1], u[:, :, :, 0], u[:, :, :, -1]])


def ghost_planes(table, index, valid, own):
    result = []
    for face in range(6):
        taken = jnp.take(table[face ^ 1], index[face], axis=-1)
        result.append(jnp.where(valid[face], taken, own[face]))
    return result


def stencil(u, ghosts, live, rates):
    lap = -6.0 * u
    lap = lap + jnp.concatenate([u[:, 1:], ghosts[1][:, None]], 1) + jnp.concatenate([ghosts[0][:, None], u[:, :-1]], 1)
    lap = lap + jnp.concatenate([u[:, :, 1:], ghosts[3][:, :, None]], 2) + jnp.concatenate([ghosts[2][:, :, None], u[:, :, :-1]], 2)
    lap = lap + jnp.concatenate([u[:, :, :, 1:], ghosts[5][:, :, :, None]], 3) + jnp.concatenate([ghosts[4][:, :, :, None], u[:, :, :, :-1]], 3)
    return u + (rates[:, None, None, None, None] * live[None, None, None, None, :]) * lap


def operate(field, conductance):
    padded = jnp.pad(field, ((1, 1), (0, 0)))
    beside = padded[2:] + padded[:-2] + jnp.roll(field, 1, 1) + jnp.roll(field, -1, 1)
    return (4.0 + conductance) * field - beside


def reference(state, counts, neighbours, rows, rates, conductance):
    slots = jnp.arange(BLOCKS, dtype=jnp.int32)
    live = (slots % NB < counts[slots // NB]).astype(jnp.float32)
    valid = neighbours >= 0
    index = jnp.where(valid, neighbours, 0).astype(jnp.int32)
    u = state
    for step in range(STEPS):
        table = planes(u)
        u = stencil(u, ghost_planes(table, index, valid, table), live, rates)
    current = jnp.sum(u[6, 0] - u[5, 0], axis=(0, 1)) / 8.0
    coupled = rows >= 0
    safe = jnp.where(coupled, rows, 0).astype(jnp.int32)
    source = jnp.zeros((NI,), jnp.float32).at[safe].add(jnp.where(coupled, current, 0.0)).reshape(NLAT, NLON)
    potential = jnp.zeros_like(source)
    residual, direction = source, source
    norm_now = jnp.sum(residual * residual)
    for step in range(ITERS):
        image = operate(direction, conductance)
        alpha = norm_now / jnp.sum(direction * image)
        potential = potential + alpha * direction
        residual = residual - alpha * image
        norm_next = jnp.sum(residual * residual)
        direction = residual + (norm_next / norm_now) * direction
        norm_now = norm_next
    added = jnp.where(coupled, potential.reshape(-1)[safe], 0.0)
    u = u.at[1, 0].add(added[None, None, :])
    return u, potential
```

```python
import functools

import jax
import jax.numpy as jnp
from jax import lax
from jax.experimental import pallas as pl
from jax.experimental.pallas import tpu as pltpu
from jax.sharding import PartitionSpec as P

ITERS = 3
EDGE = 128
FAR = 1 << 29
PAIR = 2
VMEM_LIMIT = 48 * 1024 * 1024
BF16 = jnp.bfloat16
F32 = jnp.float32


def params():
    return pltpu.CompilerParams(vmem_limit_bytes=VMEM_LIMIT)


def split(x):
    high = x.astype(BF16)
    low = (x - high.astype(F32)).astype(BF16)
    return jnp.concatenate([high, low], axis=0)


def picked(table, selector):
    rows = table.shape[0]
    both = jnp.dot(split(table), selector, preferred_element_type=F32)
    return both[:rows] + both[rows:]


def plane(ref, face):
    end = 0 if face % 2 == 0 else ref.shape[1] - 1
    if face < 2:
        return ref[:, end]
    if face < 4:
        return ref[:, :, end]
    return ref[:, :, :, end, :]


def relative(neighbours, base):
    return jnp.where(neighbours < 0, FAR, neighbours - base)


def one_hot(index, depth):
    rows = lax.broadcasted_iota(jnp.int32, (depth, index.shape[-1]), 0)
    return jnp.where(rows == index, 1.0, 0.0).astype(BF16)


def write_edges(ref, count, head_ref, tail_ref):
    slots = ref.shape[-1]
    lane = lax.broadcasted_iota(jnp.int32, (1, EDGE), 1)
    late = lane + (slots - EDGE) < count
    for face in range(6):
        cells = plane(ref, face)
        head_ref[face] = cells[..., :EDGE]
        tail_ref[face] = jnp.where(
            late, cells[..., slots - EDGE :], cells[..., slots - 2 * EDGE : slots - EDGE]
        )


def edges_kernel(count_ref, u_ref, head_ref, tail_ref):
    write_edges(u_ref, count_ref[0], head_ref, tail_ref)


def step_size(rates_ref, count_ref, var, slots):
    live = lax.broadcasted_iota(jnp.int32, (1, slots), 1) < count_ref[0]
    return jnp.where(live, rates_ref[var], 0.0)


def local_kernel(base_ref, count_ref, rates_ref, near_ref, u_ref, out_ref, selector, ghosts):
    pair, size, _, _, slots = u_ref.shape

    @pl.when(pl.program_id(0) == 0)
    def _():
        for face in range(6):
            index = relative(near_ref[face : face + 1, :], base_ref[0])
            selector[face] = one_hot(index, slots)

    for face in range(6):
        table = plane(u_ref, face ^ 1).reshape(pair * size * size, slots)
        taken = picked(table, selector[face]).reshape(pair, size, size, slots)
        outer = near_ref[face : face + 1, :] < 0
        ghosts[face] = jnp.where(outer, plane(u_ref, face), taken)

    row = lax.broadcasted_iota(jnp.int32, (size, slots), 0)
    first, last = row == 0, row == size - 1

    def variable(v, carry):
        factor = step_size(rates_ref, count_ref, pl.program_id(0) * pair + v, slots)
        for i in range(size):
            for j in range(size):
                cell = u_ref[v, i, j]
                above = u_ref[v, i + 1, j] if i < size - 1 else ghosts[1, v, j]
                below = u_ref[v, i - 1, j] if i > 0 else ghosts[0, v, j]
                right = u_ref[v, i, j + 1] if j < size - 1 else ghosts[3, v, i]
                left = u_ref[v, i, j - 1] if j > 0 else ghosts[2, v, i]
                front = jnp.where(last, ghosts[5, v, i, j : j + 1, :], pltpu.roll(cell, size - 1, 0))
                back = jnp.where(first, ghosts[4, v, i, j : j + 1, :], pltpu.roll(cell, 1, 0))
                lap = ((above + below) + (right + left)) + ((front + back) - 6.0 * cell)
                out_ref[v, i, j] = cell + factor * lap
        return carry

    lax.fori_loop(0, pair, variable, 0)


def remote_body(base_ref, count_ref, rates_ref, near_ref, lower_ref, upper_ref, u_ref, out_ref, selector, ghosts):
    pair, size, _, _, slots = u_ref.shape

    @pl.when(pl.program_id(0) == 0)
    def _():
        for face in range(6):
            index = relative(near_ref[face : face + 1, :], base_ref[0])
            below = jnp.where(index < 0, index & (EDGE - 1), -1)
            beyond = (index >= slots) & (index < FAR)
            index = jnp.where(beyond, index - slots + EDGE, below)
            selector[face] = one_hot(index, 2 * EDGE)

    for face in range(6):
        lower = lower_ref[face ^ 1].reshape(pair * size * size, EDGE)
        upper = upper_ref[face ^ 1].reshape(pair * size * size, EDGE)
        table = jnp.concatenate([lower, upper], axis=1)
        ghosts[face] = picked(table, selector[face]).reshape(pair, size, size, slots)

    row = lax.broadcasted_iota(jnp.int32, (size, slots), 0)
    first, last = row == 0, row == size - 1

    def variable(v, carry):
        factor = step_size(rates_ref, count_ref, pl.program_id(0) * pair + v, slots)
        for i in range(size):
            for j in range(size):
                extra = jnp.where(
                    last,
                    ghosts[5, v, i, j : j + 1, :],
                    jnp.where(first, ghosts[4, v, i, j : j + 1, :], 0.0),
                )
                if i == 0:
                    extra = extra + ghosts[0, v, j]
                if i == size - 1:
                    extra = extra + ghosts[1, v, j]
                if j == 0:
                    extra = extra + ghosts[2, v, i]
                if j == size - 1:
                    extra = extra + ghosts[3, v, i]
                out_ref[v, i, j] = u_ref[v, i, j] + factor * extra
        return carry

    lax.fori_loop(0, pair, variable, 0)


def remote_edges_kernel(base_ref, count_ref, rates_ref, near_ref, lower_ref, upper_ref, u_ref,
                        out_ref, head_ref, tail_ref, selector, ghosts):
    remote_body(base_ref, count_ref, rates_ref, near_ref, lower_ref, upper_ref, u_ref, out_ref, selector, ghosts)
    write_edges(out_ref, count_ref[0], head_ref, tail_ref)


def remote_sums_kernel(base_ref, count_ref, rates_ref, near_ref, lower_ref, upper_ref, u_ref,
                       out_ref, sums_ref, selector, ghosts):
    remote_body(base_ref, count_ref, rates_ref, near_ref, lower_ref, upper_ref, u_ref, out_ref, selector, ghosts)
    for v in range(out_ref.shape[0]):
        sums_ref[0, v : v + 1, :] = jnp.sum(jnp.sum(out_ref[v, 0], axis=0), axis=0, keepdims=True)


def total(x):
    return jnp.sum(x, axis=(0, 1), keepdims=True)


def grid_kernel(shift, first_ref, cells_ref, currents_ref, cond_ref, rows_ref, u_ref, out_ref, share_ref, held):
    lats, lons = cond_ref.shape
    chunks, chunk = cells_ref.shape
    mask = lons - 1

    def gathered(c, acc):
        cell = cells_ref[pl.ds(c, 1), :]
        current = currents_ref[pl.ds(c, 1), :]
        lat = cell >> shift
        lon = cell & mask
        here = lax.broadcasted_iota(jnp.int32, (lats, chunk), 0) == lat
        high = current.astype(BF16).astype(F32)
        low = current - high
        weighted = jnp.concatenate(
            [jnp.where(here, high, 0.0).astype(BF16), jnp.where(here, low, 0.0).astype(BF16)], axis=0
        )
        across = one_hot(lon, lons)
        return acc + lax.dot_general(weighted, across, (((1,), (1,)), ((), ())), preferred_element_type=F32)

    acc = lax.fori_loop(0, chunks, gathered, jnp.zeros((2 * lats, lons), F32))
    source = acc[:lats] + acc[lats:]

    weight = 4.0 + cond_ref[...]
    row = lax.broadcasted_iota(jnp.int32, (lats, lons), 0)
    potential = jnp.zeros_like(source)
    residual = source
    direction = source
    now = total(residual * residual)
    for _ in range(ITERS):
        south = jnp.where(row == 0, 0.0, pltpu.roll(direction, 1, 0))
        north = jnp.where(row == lats - 1, 0.0, pltpu.roll(direction, lats - 1, 0))
        beside = south + north + pltpu.roll(direction, 1, 1) + pltpu.roll(direction, lons - 1, 1)
        image = weight * direction - beside
        alpha = now / total(direction * image)
        potential = potential + alpha * direction
        residual = residual - alpha * image
        new = total(residual * residual)
        direction = residual + (new / now) * direction
        now = new

    held[...] = potential
    for r in range(share_ref.shape[0]):
        share_ref[r : r + 1, :] = held[pl.ds(first_ref[0] + r, 1), :]
    own = rows_ref[...]
    across = picked(potential, one_hot(jnp.where(own < 0, -1, own & mask), lons))
    here = lax.broadcasted_iota(jnp.int32, across.shape, 0) == (own >> shift)
    added = jnp.sum(jnp.where(here, across, 0.0), axis=0, keepdims=True)
    out_ref[...] = u_ref[...] + added


def smem():
    return pl.BlockSpec(memory_space=pltpu.SMEM)


def on_device(state, counts, neighbours, rows, rates, conductance):
    vars_, size, _, _, slots = state.shape
    axes = ("grp", "blk")
    groups, blks = lax.axis_size("grp"), lax.axis_size("blk")
    devices = groups * blks
    blk = lax.axis_index("blk")
    device = lax.axis_index("grp") * blks + blk
    base = jnp.reshape(device * slots, (1,)).astype(jnp.int32)
    grid = (vars_ // PAIR,)
    block = pl.BlockSpec((PAIR, size, size, size, slots), lambda g: (g, 0, 0, 0, 0))
    edge = pl.BlockSpec((6, PAIR, size, size, EDGE), lambda g: (0, g, 0, 0, 0))
    near = pl.BlockSpec(neighbours.shape, lambda g: (0, 0))
    sums = pl.BlockSpec((1, PAIR, slots), lambda g: (g, 0, 0))
    whole = jax.ShapeDtypeStruct(state.shape, F32)
    edge_shape = jax.ShapeDtypeStruct((6, vars_, size, size, EDGE), F32)
    sums_shape = jax.ShapeDtypeStruct((vars_ // PAIR, PAIR, slots), F32)
    ghosts = pltpu.VMEM((6, PAIR, size, size, slots), F32)
    up = [(d, d + 1) for d in range(devices - 1)]
    down = [(d + 1, d) for d in range(devices - 1)]

    def exchange(head, tail):
        return lax.ppermute(tail, axes, up), lax.ppermute(head, axes, down)

    def local(u):
        return pl.pallas_call(
            local_kernel,
            grid=grid,
            in_specs=[smem(), smem(), smem(), near, block],
            out_specs=block,
            out_shape=whole,
            scratch_shapes=[pltpu.VMEM((6, slots, slots), BF16), ghosts],
            compiler_params=params(),
            cost_estimate=pl.CostEstimate(flops=10 * 10**9, bytes_accessed=2 * u.size * 4, transcendentals=0),
            name="local_step",
        )(base, counts, rates, neighbours, u)

    def remote(kernel, u, lower, upper, out_specs, out_shape):
        return pl.pallas_call(
            kernel,
            grid=grid,
            in_specs=[smem(), smem(), smem(), near, edge, edge, block],
            out_specs=[block] + out_specs,
            out_shape=[whole] + out_shape,
            scratch_shapes=[pltpu.VMEM((6, 2 * EDGE, slots), BF16), ghosts],
            compiler_params=params(),
            cost_estimate=pl.CostEstimate(flops=5 * 10**9, bytes_accessed=2 * u.size * 4, transcendentals=0),
            name="remote_step",
        )(base, counts, rates, neighbours, lower, upper, u)

    cells = lax.all_gather(rows, axes, axis=0, tiled=True)
    conduct = lax.all_gather(conductance, "blk", axis=0, tiled=True)

    head, tail = pl.pallas_call(
        edges_kernel,
        grid=grid,
        in_specs=[smem(), block],
        out_specs=[edge, edge],
        out_shape=[edge_shape, edge_shape],
        compiler_params=params(),
        name="edges",
    )(counts, state)
    lower, upper = exchange(head, tail)
    u = local(state)
    u, head, tail = remote(remote_edges_kernel, u, lower, upper, [edge, edge], [edge_shape, edge_shape])
    lower, upper = exchange(head, tail)
    u = local(u)
    u, faces = remote(remote_sums_kernel, u, lower, upper, [sums], [sums_shape])
    faces = faces.reshape(vars_, slots)
    current = (faces[6] - faces[5]) / 8.0
    currents = lax.all_gather(current, axes, axis=0, tiled=True)

    lat_rows, lons = conductance.shape
    chunk = 4 * slots
    first = jnp.reshape(blk * lat_rows, (1,)).astype(jnp.int32)
    face = pl.BlockSpec((1, 1, size, size, slots), lambda g: (1, 0, 0, 0, 0))

    def full(*shape):
        return pl.BlockSpec(shape, lambda g: (0,) * len(shape))

    lats = conduct.shape[0]
    u, share = pl.pallas_call(
        functools.partial(grid_kernel, lons.bit_length() - 1),
        grid=(1,),
        in_specs=[
            smem(),
            full(devices * slots // chunk, chunk),
            full(devices * slots // chunk, chunk),
            full(lats, lons),
            full(1, slots),
            face,
        ],
        out_specs=[face, full(lat_rows, lons)],
        out_shape=[whole, jax.ShapeDtypeStruct(conductance.shape, F32)],
        scratch_shapes=[pltpu.VMEM((lats, lons), F32)],
        input_output_aliases={5: 0},
        compiler_params=params(),
        name="ionosphere",
    )(first, cells.reshape(-1, chunk), currents.reshape(-1, chunk), conduct, rows.reshape(1, slots), u)
    return (u, share)


def solution(mesh):
    placed = (
        P(None, None, None, None, ("grp", "blk")),
        P(("grp", "blk")),
        P(None, ("grp", "blk")),
        P(("grp", "blk")),
        P(),
        P("blk", None),
    )
    return jax.shard_map(
        on_device,
        mesh=mesh,
        in_specs=placed,
        out_specs=(P(None, None, None, None, ("grp", "blk")), P("blk", None)),
        check_vma=False,
    )
```

```python
import functools

import jax
import jax.numpy as jnp
from jax import lax
from jax.experimental import pallas as pl
from jax.experimental.pallas import tpu as pltpu
from jax.sharding import PartitionSpec as P

ITERS = 3
EDGE = 128
FAR = 1 << 29
PAIR = 2
VMEM_LIMIT = 48 * 1024 * 1024
BF16 = jnp.bfloat16
F32 = jnp.float32


def params():
    return pltpu.CompilerParams(vmem_limit_bytes=VMEM_LIMIT)


def split(x):
    high = x.astype(BF16)
    low = (x - high.astype(F32)).astype(BF16)
    return jnp.concatenate([high, low], axis=0)


def picked(table, selector):
    rows = table.shape[0]
    both = jnp.dot(split(table), selector, preferred_element_type=F32)
    return both[:rows] + both[rows:]


def plane(ref, face):
    end = 0 if face % 2 == 0 else ref.shape[1] - 1
    if face < 2:
        return ref[:, end]
    if face < 4:
        return ref[:, :, end]
    return ref[:, :, :, end, :]


def relative(neighbours, base):
    return jnp.where(neighbours < 0, FAR, neighbours - base)


def one_hot(index, depth):
    rows = lax.broadcasted_iota(jnp.int32, (depth, index.shape[-1]), 0)
    return jnp.where(rows == index, 1.0, 0.0).astype(BF16)


def write_edges(ref, count, head_ref, tail_ref):
    slots = ref.shape[-1]
    lane = lax.broadcasted_iota(jnp.int32, (1, EDGE), 1)
    late = lane + (slots - EDGE) < count
    for face in range(6):
        cells = plane(ref, face)
        head_ref[face] = cells[..., :EDGE]
        tail_ref[face] = jnp.where(
            late, cells[..., slots - EDGE :], cells[..., slots - 2 * EDGE : slots - EDGE]
        )


def edges_kernel(count_ref, u_ref, head_ref, tail_ref):
    write_edges(u_ref, count_ref[0], head_ref, tail_ref)


def step_size(rates_ref, count_ref, var, slots):
    live = lax.broadcasted_iota(jnp.int32, (1, slots), 1) < count_ref[0]
    return jnp.where(live, rates_ref[var], 0.0)


def local_kernel(base_ref, count_ref, rates_ref, near_ref, u_ref, out_ref, selector, ghosts):
    pair, size, _, _, slots = u_ref.shape

    @pl.when(pl.program_id(0) == 0)
    def _():
        for face in range(6):
            index = relative(near_ref[face : face + 1, :], base_ref[0])
            selector[face] = one_hot(index, slots)

    for face in range(6):
        table = plane(u_ref, face ^ 1).reshape(pair * size * size, slots)
        taken = picked(table, selector[face]).reshape(pair, size, size, slots)
        outer = near_ref[face : face + 1, :] < 0
        ghosts[face] = jnp.where(outer, plane(u_ref, face), taken)

    row = lax.broadcasted_iota(jnp.int32, (size, slots), 0)
    first, last = row == 0, row == size - 1

    def variable(v, carry):
        factor = step_size(rates_ref, count_ref, pl.program_id(0) * pair + v, slots)
        for i in range(size):
            for j in range(size):
                cell = u_ref[v, i, j]
                above = u_ref[v, i + 1, j] if i < size - 1 else ghosts[1, v, j]
                below = u_ref[v, i - 1, j] if i > 0 else ghosts[0, v, j]
                right = u_ref[v, i, j + 1] if j < size - 1 else ghosts[3, v, i]
                left = u_ref[v, i, j - 1] if j > 0 else ghosts[2, v, i]
                front = jnp.where(last, ghosts[5, v, i, j : j + 1, :], pltpu.roll(cell, size - 1, 0))
                back = jnp.where(first, ghosts[4, v, i, j : j + 1, :], pltpu.roll(cell, 1, 0))
                lap = ((above + below) + (right + left)) + ((front + back) - 6.0 * cell)
                out_ref[v, i, j] = cell + factor * lap
        return carry

    lax.fori_loop(0, pair, variable, 0)


def remote_body(base_ref, count_ref, rates_ref, near_ref, lower_ref, upper_ref, u_ref, out_ref, selector, ghosts):
    pair, size, _, _, slots = u_ref.shape

    @pl.when(pl.program_id(0) == 0)
    def _():
        for face in range(6):
            index = relative(near_ref[face : face + 1, :], base_ref[0])
            below = jnp.where(index < 0, index & (EDGE - 1), -1)
            beyond = (index >= slots) & (index < FAR)
            index = jnp.where(beyond, index - slots + EDGE, below)
            selector[face] = one_hot(index, 2 * EDGE)

    for face in range(6):
        lower = lower_ref[face ^ 1].reshape(pair * size * size, EDGE)
        upper = upper_ref[face ^ 1].reshape(pair * size * size, EDGE)
        table = jnp.concatenate([lower, upper], axis=1)
        ghosts[face] = picked(table, selector[face]).reshape(pair, size, size, slots)

    row = lax.broadcasted_iota(jnp.int32, (size, slots), 0)
    first, last = row == 0, row == size - 1

    def variable(v, carry):
        factor = step_size(rates_ref, count_ref, pl.program_id(0) * pair + v, slots)
        for i in range(size):
            for j in range(size):
                extra = jnp.where(
                    last,
                    ghosts[5, v, i, j : j + 1, :],
                    jnp.where(first, ghosts[4, v, i, j : j + 1, :], 0.0),
                )
                if i == 0:
                    extra = extra + ghosts[0, v, j]
                if i == size - 1:
                    extra = extra + ghosts[1, v, j]
                if j == 0:
                    extra = extra + ghosts[2, v, i]
                if j == size - 1:
                    extra = extra + ghosts[3, v, i]
                out_ref[v, i, j] = u_ref[v, i, j] + factor * extra
        return carry

    lax.fori_loop(0, pair, variable, 0)


def remote_edges_kernel(base_ref, count_ref, rates_ref, near_ref, lower_ref, upper_ref, u_ref,
                        out_ref, head_ref, tail_ref, selector, ghosts):
    remote_body(base_ref, count_ref, rates_ref, near_ref, lower_ref, upper_ref, u_ref, out_ref, selector, ghosts)
    write_edges(out_ref, count_ref[0], head_ref, tail_ref)


def remote_sums_kernel(base_ref, count_ref, rates_ref, near_ref, lower_ref, upper_ref, u_ref,
                       out_ref, sums_ref, selector, ghosts):
    remote_body(base_ref, count_ref, rates_ref, near_ref, lower_ref, upper_ref, u_ref, out_ref, selector, ghosts)
    for v in range(out_ref.shape[0]):
        sums_ref[0, v : v + 1, :] = jnp.sum(jnp.sum(out_ref[v, 0], axis=0), axis=0, keepdims=True)


def total(x):
    return jnp.sum(x, axis=(0, 1), keepdims=True)


def spread_kernel(groups, blks, rows_ref, faces_ref, cond_ref, parts_ref, whole_ref,
                  packet, landed, slabs, send_sem, recv_sem, slab_send_sem, slab_recv_sem):
    devices = groups * blks
    grp, blk = lax.axis_index("grp"), lax.axis_index("blk")
    me = grp * blks + blk

    def place(step):
        other = lax.rem(me + step, devices)
        return (other // blks, lax.rem(other, blks))

    def along(step):
        return (grp, lax.rem(blk + step, blks))

    barrier = pltpu.get_barrier_semaphore()

    def greet(step, carry):
        pl.semaphore_signal(barrier, inc=1, device_id=place(step), device_id_type=pl.DeviceIdType.MESH)
        return carry

    lax.fori_loop(1, devices, greet, 0)
    packet[0:1, :] = rows_ref[...].astype(F32)
    packet[1:2, :] = (faces_ref[6:7, :] - faces_ref[5:6, :]) / 8.0
    pl.semaphore_wait(barrier, devices - 1)

    def copy(step):
        return pltpu.make_async_remote_copy(
            src_ref=packet, dst_ref=landed.at[me], send_sem=send_sem.at[step], recv_sem=recv_sem.at[step],
            device_id=place(step), device_id_type=pl.DeviceIdType.MESH)

    def slab_copy(step):
        return pltpu.make_async_remote_copy(
            src_ref=cond_ref, dst_ref=slabs.at[blk], send_sem=slab_send_sem.at[step],
            recv_sem=slab_recv_sem.at[step], device_id=along(step), device_id_type=pl.DeviceIdType.MESH)

    def start(step, carry):
        copy(step).start()
        return carry

    def start_slab(step, carry):
        slab_copy(step).start()
        return carry

    def finish(step, carry):
        copy(step).wait()
        return carry

    def finish_slab(step, carry):
        slab_copy(step).wait()
        return carry

    lax.fori_loop(1, devices, start, 0)
    lax.fori_loop(1, blks, start_slab, 0)
    landed[me] = packet[...]
    slabs[blk] = cond_ref[...]
    lax.fori_loop(1, devices, finish, 0)
    lax.fori_loop(1, blks, finish_slab, 0)
    parts_ref[...] = landed[...]
    lats = cond_ref.shape[0]
    for b in range(blks):
        whole_ref[b * lats : (b + 1) * lats, :] = slabs[b]


def grid_kernel(shift, first_ref, parts_ref, cond_ref, rows_ref, u_ref, out_ref, share_ref, held):
    lats, lons = cond_ref.shape
    devices, _, slots = parts_ref.shape
    mask = lons - 1

    def gathered(c, acc):
        for part in range(4):
            piece = parts_ref[c * 4 + part]
            cell = piece[0:1, :].astype(jnp.int32)
            current = piece[1:2, :]
            here = lax.broadcasted_iota(jnp.int32, (lats, slots), 0) == (cell >> shift)
            high = current.astype(BF16).astype(F32)
            low = current - high
            weighted = jnp.concatenate(
                [jnp.where(here, high, 0.0).astype(BF16), jnp.where(here, low, 0.0).astype(BF16)], axis=0
            )
            across = one_hot(cell & mask, lons)
            acc = acc + lax.dot_general(
                weighted, across, (((1,), (1,)), ((), ())), preferred_element_type=F32)
        return acc

    acc = lax.fori_loop(0, devices // 4, gathered, jnp.zeros((2 * lats, lons), F32))
    source = acc[:lats] + acc[lats:]

    weight = 4.0 + cond_ref[...]
    row = lax.broadcasted_iota(jnp.int32, (lats, lons), 0)
    potential = jnp.zeros_like(source)
    residual = source
    direction = source
    now = total(residual * residual)
    for _ in range(ITERS):
        south = jnp.where(row == 0, 0.0, pltpu.roll(direction, 1, 0))
        north = jnp.where(row == lats - 1, 0.0, pltpu.roll(direction, lats - 1, 0))
        beside = south + north + pltpu.roll(direction, 1, 1) + pltpu.roll(direction, lons - 1, 1)
        image = weight * direction - beside
        alpha = now / total(direction * image)
        potential = potential + alpha * direction
        residual = residual - alpha * image
        new = total(residual * residual)
        direction = residual + (new / now) * direction
        now = new

    held[...] = potential
    for r in range(share_ref.shape[0]):
        share_ref[r : r + 1, :] = held[pl.ds(first_ref[0] + r, 1), :]
    own = rows_ref[...]
    across = picked(potential, one_hot(jnp.where(own < 0, -1, own & mask), lons))
    here = lax.broadcasted_iota(jnp.int32, across.shape, 0) == (own >> shift)
    added = jnp.sum(jnp.where(here, across, 0.0), axis=0, keepdims=True)
    out_ref[...] = u_ref[...] + added


def smem():
    return pl.BlockSpec(memory_space=pltpu.SMEM)


def on_device(state, counts, neighbours, rows, rates, conductance):
    vars_, size, _, _, slots = state.shape
    axes = ("grp", "blk")
    groups, blks = lax.axis_size("grp"), lax.axis_size("blk")
    devices = groups * blks
    blk = lax.axis_index("blk")
    device = lax.axis_index("grp") * blks + blk
    base = jnp.reshape(device * slots, (1,)).astype(jnp.int32)
    grid = (vars_ // PAIR,)
    block = pl.BlockSpec((PAIR, size, size, size, slots), lambda g: (g, 0, 0, 0, 0))
    edge = pl.BlockSpec((6, PAIR, size, size, EDGE), lambda g: (0, g, 0, 0, 0))
    near = pl.BlockSpec(neighbours.shape, lambda g: (0, 0))
    sums = pl.BlockSpec((1, PAIR, slots), lambda g: (g, 0, 0))
    whole = jax.ShapeDtypeStruct(state.shape, F32)
    edge_shape = jax.ShapeDtypeStruct((6, vars_, size, size, EDGE), F32)
    sums_shape = jax.ShapeDtypeStruct((vars_ // PAIR, PAIR, slots), F32)
    ghosts = pltpu.VMEM((6, PAIR, size, size, slots), F32)
    up = [(d, d + 1) for d in range(devices - 1)]
    down = [(d + 1, d) for d in range(devices - 1)]

    def exchange(head, tail):
        return lax.ppermute(tail, axes, up), lax.ppermute(head, axes, down)

    def local(u):
        return pl.pallas_call(
            local_kernel,
            grid=grid,
            in_specs=[smem(), smem(), smem(), near, block],
            out_specs=block,
            out_shape=whole,
            scratch_shapes=[pltpu.VMEM((6, slots, slots), BF16), ghosts],
            compiler_params=params(),
            cost_estimate=pl.CostEstimate(flops=10 * 10**9, bytes_accessed=2 * u.size * 4, transcendentals=0),
            name="local_step",
        )(base, counts, rates, neighbours, u)

    def remote(kernel, u, lower, upper, out_specs, out_shape):
        return pl.pallas_call(
            kernel,
            grid=grid,
            in_specs=[smem(), smem(), smem(), near, edge, edge, block],
            out_specs=[block] + out_specs,
            out_shape=[whole] + out_shape,
            scratch_shapes=[pltpu.VMEM((6, 2 * EDGE, slots), BF16), ghosts],
            compiler_params=params(),
            cost_estimate=pl.CostEstimate(flops=5 * 10**9, bytes_accessed=2 * u.size * 4, transcendentals=0),
            name="remote_step",
        )(base, counts, rates, neighbours, lower, upper, u)

    head, tail = pl.pallas_call(
        edges_kernel,
        grid=grid,
        in_specs=[smem(), block],
        out_specs=[edge, edge],
        out_shape=[edge_shape, edge_shape],
        compiler_params=params(),
        name="edges",
    )(counts, state)
    lower, upper = exchange(head, tail)
    u = local(state)
    u, head, tail = remote(remote_edges_kernel, u, lower, upper, [edge, edge], [edge_shape, edge_shape])
    lower, upper = exchange(head, tail)
    u = local(u)
    u, faces = remote(remote_sums_kernel, u, lower, upper, [sums], [sums_shape])
    lat_rows, lons = conductance.shape
    lats = lat_rows * blks
    own_rows = rows.reshape(1, slots)
    parts, conduct = pl.pallas_call(
        functools.partial(spread_kernel, groups, blks),
        in_specs=[pl.BlockSpec(memory_space=pltpu.VMEM)] * 3,
        out_specs=[pl.BlockSpec(memory_space=pltpu.VMEM)] * 2,
        out_shape=[jax.ShapeDtypeStruct((devices, 2, slots), F32), jax.ShapeDtypeStruct((lats, lons), F32)],
        scratch_shapes=[
            pltpu.VMEM((2, slots), F32),
            pltpu.VMEM((devices, 2, slots), F32),
            pltpu.VMEM((blks, lat_rows, lons), F32),
            pltpu.SemaphoreType.DMA((devices,)),
            pltpu.SemaphoreType.DMA((devices,)),
            pltpu.SemaphoreType.DMA((blks,)),
            pltpu.SemaphoreType.DMA((blks,)),
        ],
        compiler_params=pltpu.CompilerParams(
            vmem_limit_bytes=VMEM_LIMIT, collective_id=0, has_side_effects=True),
        name="spread",
    )(own_rows, faces.reshape(vars_, slots), conductance)

    first = jnp.reshape(blk * lat_rows, (1,)).astype(jnp.int32)
    face = pl.BlockSpec((1, 1, size, size, slots), lambda g: (1, 0, 0, 0, 0))

    def full(*shape):
        return pl.BlockSpec(shape, lambda g: (0,) * len(shape))

    u, share = pl.pallas_call(
        functools.partial(grid_kernel, lons.bit_length() - 1),
        grid=(1,),
        in_specs=[
            smem(),
            full(devices, 2, slots),
            full(lats, lons),
            full(1, slots),
            face,
        ],
        out_specs=[face, full(lat_rows, lons)],
        out_shape=[whole, jax.ShapeDtypeStruct(conductance.shape, F32)],
        scratch_shapes=[pltpu.VMEM((lats, lons), F32)],
        input_output_aliases={4: 0},
        compiler_params=params(),
        name="ionosphere",
    )(first, parts, conduct, own_rows, u)
    return (u, share)


def solution(mesh):
    placed = (
        P(None, None, None, None, ("grp", "blk")),
        P(("grp", "blk")),
        P(None, ("grp", "blk")),
        P(("grp", "blk")),
        P(),
        P("blk", None),
    )
    return jax.shard_map(
        on_device,
        mesh=mesh,
        in_specs=placed,
        out_specs=(P(None, None, None, None, ("grp", "blk")), P("blk", None)),
        check_vma=False,
    )
```

```python
import functools

import jax
import jax.numpy as jnp
from jax import lax
from jax.experimental import pallas as pl
from jax.experimental.pallas import tpu as pltpu
from jax.sharding import PartitionSpec as P

ITERS = 3
EDGE = 128
FAR = 1 << 29
PAIR = 2
VMEM_LIMIT = 48 * 1024 * 1024
BF16 = jnp.bfloat16
F32 = jnp.float32


def params():
    return pltpu.CompilerParams(vmem_limit_bytes=VMEM_LIMIT)


def split(x):
    high = x.astype(BF16)
    low = (x - high.astype(F32)).astype(BF16)
    return jnp.concatenate([high, low], axis=0)


def picked(table, selector):
    rows = table.shape[0]
    both = jnp.dot(split(table), selector, preferred_element_type=F32)
    return both[:rows] + both[rows:]


def plane(ref, face):
    end = 0 if face % 2 == 0 else ref.shape[1] - 1
    if face < 2:
        return ref[:, end]
    if face < 4:
        return ref[:, :, end]
    return ref[:, :, :, end, :]


def one_hot(index, depth):
    rows = lax.broadcasted_iota(jnp.int32, (depth, index.shape[-1]), 0)
    return jnp.where(rows == index, 1.0, 0.0).astype(BF16)


def write_edges(ref, count, head_ref, tail_ref):
    size, slots = ref.shape[1], ref.shape[-1]
    lane = lax.broadcasted_iota(jnp.int32, (1, EDGE), 1)
    late = lane + (slots - EDGE) < count
    at = 0
    for face in range(6):
        cells = plane(ref, face)
        if face >= 2:
            cells = cells[:, 1 : size - 1]
        tiles = cells.shape[1]
        head_ref[:, at : at + tiles] = cells[..., :EDGE]
        tail_ref[:, at : at + tiles] = jnp.where(
            late, cells[..., slots - EDGE :], cells[..., slots - 2 * EDGE : slots - EDGE]
        )
        at += tiles


def read_edges(ref, face):
    size = ref.shape[2]
    end = 0 if face % 2 == 0 else size - 1
    if face < 2:
        return ref[:, face * size : (face + 1) * size]
    at = 2 * size + (face - 2) * (size - 2)
    middle = ref[:, at : at + size - 2]
    if face < 4:
        first, last = ref[:, end : end + 1], ref[:, size + end : size + end + 1]
    else:
        first = ref[:, 0:size, end, :][:, None]
        last = ref[:, size : 2 * size, end, :][:, None]
    return jnp.concatenate([first, middle, last], axis=1)


def edges_kernel(count_ref, u_ref, *refs):
    head_ref, tail_ref = refs[-2:]
    write_edges(u_ref, count_ref[0], head_ref, tail_ref)


def step_body(start, base_ref, count_ref, rates_ref, near_ref, lower_ref, upper_ref, u_ref, out_ref, selector, ghosts):
    pair, size, _, _, slots = u_ref.shape

    @pl.when(pl.program_id(0) == 0)
    def _():
        for face in range(6):
            index = near_ref[face : face + 1, :]
            index = jnp.where(index < 0, FAR, index - base_ref[0])
            index = jnp.where(
                index < 0,
                slots + (index & (EDGE - 1)),
                jnp.where(index >= slots, index + EDGE, index),
            )
            selector[face] = one_hot(index, slots + 2 * EDGE)

    for face in range(6):
        rows = pair * size * size
        table = jnp.concatenate(
            [
                plane(u_ref, face ^ 1).reshape(rows, slots),
                read_edges(lower_ref, face ^ 1).reshape(rows, EDGE),
                read_edges(upper_ref, face ^ 1).reshape(rows, EDGE),
            ],
            axis=1,
        )
        taken = picked(table, selector[face]).reshape(pair, size, size, slots)
        outer = near_ref[face : face + 1, :] < 0
        ghosts[face] = jnp.where(outer, plane(u_ref, face), taken)

    row = lax.broadcasted_iota(jnp.int32, (size, slots), 0)
    first, last = row == 0, row == size - 1

    def variable(v, carry):
        live = lax.broadcasted_iota(jnp.int32, (1, slots), 1) < count_ref[0]
        factor = jnp.where(live, rates_ref[start + pl.program_id(0) * pair + v], 0.0)
        for i in range(size):
            for j in range(size):
                cell = u_ref[v, i, j]
                above = u_ref[v, i + 1, j] if i < size - 1 else ghosts[1, v, j]
                below = u_ref[v, i - 1, j] if i > 0 else ghosts[0, v, j]
                right = u_ref[v, i, j + 1] if j < size - 1 else ghosts[3, v, i]
                left = u_ref[v, i, j - 1] if j > 0 else ghosts[2, v, i]
                front = jnp.where(last, ghosts[5, v, i, j : j + 1, :], pltpu.roll(cell, size - 1, 0))
                back = jnp.where(first, ghosts[4, v, i, j : j + 1, :], pltpu.roll(cell, 1, 0))
                lap = ((above + below) + (right + left)) + ((front + back) - 6.0 * cell)
                out_ref[v, i, j] = cell + factor * lap
        return carry

    lax.fori_loop(0, pair, variable, 0)


def edge_step_kernel(start, base_ref, count_ref, rates_ref, near_ref, lower_ref, upper_ref, u_ref, *refs):
    out_ref, head_ref, tail_ref, selector, ghosts = refs[-5:]
    step_body(start, base_ref, count_ref, rates_ref, near_ref, lower_ref, upper_ref, u_ref, out_ref, selector, ghosts)
    write_edges(out_ref, count_ref[0], head_ref, tail_ref)


def sum_step_kernel(start, base_ref, count_ref, rates_ref, near_ref, lower_ref, upper_ref, u_ref, *refs):
    out_ref, sums_ref, selector, ghosts = refs[-4:]
    step_body(start, base_ref, count_ref, rates_ref, near_ref, lower_ref, upper_ref, u_ref, out_ref, selector, ghosts)
    for v in range(out_ref.shape[0]):
        sums_ref[0, v : v + 1, :] = jnp.sum(jnp.sum(out_ref[v, 0], axis=0), axis=0, keepdims=True)


def last_step_kernel(start, base_ref, count_ref, rates_ref, near_ref, lower_ref, upper_ref, u_ref, *refs):
    added_ref = refs[0]
    out_ref, selector, ghosts = refs[-3:]
    step_body(start, base_ref, count_ref, rates_ref, near_ref, lower_ref, upper_ref, u_ref, out_ref, selector, ghosts)

    @pl.when(pl.program_id(0) == 0)
    def _():
        out_ref[1, 0] = out_ref[1, 0] + added_ref[...]


def total(x):
    return jnp.sum(x, axis=(0, 1), keepdims=True)


def spread_kernel(groups, blks, rows_ref, faces_ref, cond_ref, parts_ref, whole_ref,
                  packet, landed, slabs, send_sem, recv_sem, slab_send_sem, slab_recv_sem):
    devices = groups * blks
    grp, blk = lax.axis_index("grp"), lax.axis_index("blk")
    me = grp * blks + blk

    def place(step):
        other = lax.rem(me + step, devices)
        return (other // blks, lax.rem(other, blks))

    def along(step):
        return (grp, lax.rem(blk + step, blks))

    barrier = pltpu.get_barrier_semaphore()

    def greet(step, carry):
        pl.semaphore_signal(barrier, inc=1, device_id=place(step), device_id_type=pl.DeviceIdType.MESH)
        return carry

    lax.fori_loop(1, devices, greet, 0)
    packet[0:1, :] = rows_ref[...].astype(F32)
    packet[1:2, :] = (faces_ref[2:3, :] - faces_ref[1:2, :]) / 8.0
    pl.semaphore_wait(barrier, devices - 1)

    def copy(step):
        return pltpu.make_async_remote_copy(
            src_ref=packet, dst_ref=landed.at[me], send_sem=send_sem.at[step], recv_sem=recv_sem.at[step],
            device_id=place(step), device_id_type=pl.DeviceIdType.MESH)

    def slab_copy(step):
        return pltpu.make_async_remote_copy(
            src_ref=cond_ref, dst_ref=slabs.at[blk], send_sem=slab_send_sem.at[step],
            recv_sem=slab_recv_sem.at[step], device_id=along(step), device_id_type=pl.DeviceIdType.MESH)

    def start(step, carry):
        copy(step).start()
        return carry

    def start_slab(step, carry):
        slab_copy(step).start()
        return carry

    def finish(step, carry):
        copy(step).wait()
        return carry

    def finish_slab(step, carry):
        slab_copy(step).wait()
        return carry

    lax.fori_loop(1, devices, start, 0)
    lax.fori_loop(1, blks, start_slab, 0)
    landed[me] = packet[...]
    slabs[blk] = cond_ref[...]
    lax.fori_loop(1, devices, finish, 0)
    lax.fori_loop(1, blks, finish_slab, 0)
    parts_ref[...] = landed[...]
    lats = cond_ref.shape[0]
    for b in range(blks):
        whole_ref[b * lats : (b + 1) * lats, :] = slabs[b]


def grid_kernel(shift, first_ref, parts_ref, cond_ref, rows_ref, added_ref, share_ref, held):
    lats, lons = cond_ref.shape
    devices, _, slots = parts_ref.shape
    mask = lons - 1

    def gathered(c, acc):
        for part in range(4):
            piece = parts_ref[c * 4 + part]
            cell = piece[0:1, :].astype(jnp.int32)
            current = piece[1:2, :]
            here = lax.broadcasted_iota(jnp.int32, (lats, slots), 0) == (cell >> shift)
            high = current.astype(BF16).astype(F32)
            low = current - high
            weighted = jnp.concatenate(
                [jnp.where(here, high, 0.0).astype(BF16), jnp.where(here, low, 0.0).astype(BF16)], axis=0
            )
            across = one_hot(cell & mask, lons)
            acc = acc + lax.dot_general(
                weighted, across, (((1,), (1,)), ((), ())), preferred_element_type=F32)
        return acc

    acc = lax.fori_loop(0, devices // 4, gathered, jnp.zeros((2 * lats, lons), F32))
    source = acc[:lats] + acc[lats:]

    weight = 4.0 + cond_ref[...]
    row = lax.broadcasted_iota(jnp.int32, (lats, lons), 0)
    potential = jnp.zeros_like(source)
    residual = source
    direction = source
    now = total(residual * residual)
    for _ in range(ITERS):
        south = jnp.where(row == 0, 0.0, pltpu.roll(direction, 1, 0))
        north = jnp.where(row == lats - 1, 0.0, pltpu.roll(direction, lats - 1, 0))
        beside = south + north + pltpu.roll(direction, 1, 1) + pltpu.roll(direction, lons - 1, 1)
        image = weight * direction - beside
        alpha = now / total(direction * image)
        potential = potential + alpha * direction
        residual = residual - alpha * image
        new = total(residual * residual)
        direction = residual + (new / now) * direction
        now = new

    held[...] = potential
    for r in range(share_ref.shape[0]):
        share_ref[r : r + 1, :] = held[pl.ds(first_ref[0] + r, 1), :]
    own = rows_ref[...]
    across = picked(potential, one_hot(jnp.where(own < 0, -1, own & mask), lons))
    here = lax.broadcasted_iota(jnp.int32, across.shape, 0) == (own >> shift)
    added_ref[...] = jnp.sum(jnp.where(here, across, 0.0), axis=0, keepdims=True)


def smem():
    return pl.BlockSpec(memory_space=pltpu.SMEM)


def on_device(state, counts, neighbours, rows, rates, conductance):
    vars_, size, _, _, slots = state.shape
    axes = ("grp", "blk")
    groups, blks = lax.axis_size("grp"), lax.axis_size("blk")
    devices = groups * blks
    blk = lax.axis_index("blk")
    device = lax.axis_index("grp") * blks + blk
    base = jnp.reshape(device * slots, (1,)).astype(jnp.int32)
    half = vars_ // 2
    grid = (half // PAIR,)
    tiles = 2 * size + 4 * (size - 2)
    edge = pl.BlockSpec((PAIR, tiles, size, EDGE), lambda g: (g, 0, 0, 0))
    near = pl.BlockSpec(neighbours.shape, lambda g: (0, 0))
    sums = pl.BlockSpec((1, PAIR, slots), lambda g: (g, 0, 0))
    anywhere = pl.BlockSpec(memory_space=pl.ANY)
    whole = jax.ShapeDtypeStruct(state.shape, F32)
    part = jax.ShapeDtypeStruct((half,) + state.shape[1:], F32)
    edge_shape = jax.ShapeDtypeStruct((half, tiles, size, EDGE), F32)
    sums_shape = jax.ShapeDtypeStruct((half // PAIR, PAIR, slots), F32)
    up = [(d, d + 1) for d in range(devices - 1)]
    down = [(d + 1, d) for d in range(devices - 1)]

    def block(start):
        return pl.BlockSpec((PAIR, size, size, size, slots), lambda g: (g + start // PAIR, 0, 0, 0, 0))

    def exchange(head, tail):
        return lax.ppermute(tail, axes, up), lax.ppermute(head, axes, down)

    def edges(start, *after):
        return pl.pallas_call(
            edges_kernel,
            grid=grid,
            in_specs=[smem(), block(start)] + [anywhere] * len(after),
            out_specs=[edge, edge],
            out_shape=[edge_shape, edge_shape],
            compiler_params=params(),
            cost_estimate=pl.CostEstimate(flops=10**6, bytes_accessed=8 * 10**6, transcendentals=0),
            name="edges",
        )(counts, state, *after)

    def step(kernel, start, u, halo, out_specs, out_shape, extra=(), extra_specs=(), aliases={}):
        return pl.pallas_call(
            functools.partial(kernel, start),
            grid=grid,
            in_specs=[smem(), smem(), smem(), near, edge, edge, block(start if u is state else 0)]
            + list(extra_specs),
            out_specs=out_specs,
            out_shape=out_shape,
            scratch_shapes=[
                pltpu.VMEM((6, slots + 2 * EDGE, slots), BF16),
                pltpu.VMEM((6, PAIR, size, size, slots), F32),
            ],
            input_output_aliases=aliases,
            compiler_params=params(),
            cost_estimate=pl.CostEstimate(flops=5 * 10**9, bytes_accessed=30 * 10**6, transcendentals=0),
            name="step",
        )(base, counts, rates, neighbours, *halo, u, *extra)

    head_b, tail_b = edges(half)
    halo_b = exchange(head_b, tail_b)
    head_a, tail_a = edges(0, head_b)
    halo_a = exchange(head_a, tail_a)
    outs = [block(0), edge, edge]
    shapes = [part, edge_shape, edge_shape]
    u_b, head_b, tail_b = step(edge_step_kernel, half, state, halo_b, outs, shapes)
    halo_b = exchange(head_b, tail_b)
    u_a, head_a, tail_a = step(edge_step_kernel, 0, state, halo_a, outs, shapes, (head_b,), (anywhere,))
    halo_a = exchange(head_a, tail_a)
    u, faces = step(
        sum_step_kernel, half, u_b, halo_b, [block(half), sums], [whole, sums_shape], (head_a,), (anywhere,))

    lat_rows, lons = conductance.shape
    lats = lat_rows * blks
    own_rows = rows.reshape(1, slots)
    parts, conduct = pl.pallas_call(
        functools.partial(spread_kernel, groups, blks),
        in_specs=[pl.BlockSpec(memory_space=pltpu.VMEM)] * 3,
        out_specs=[pl.BlockSpec(memory_space=pltpu.VMEM)] * 2,
        out_shape=[jax.ShapeDtypeStruct((devices, 2, slots), F32), jax.ShapeDtypeStruct((lats, lons), F32)],
        scratch_shapes=[
            pltpu.VMEM((2, slots), F32),
            pltpu.VMEM((devices, 2, slots), F32),
            pltpu.VMEM((blks, lat_rows, lons), F32),
            pltpu.SemaphoreType.DMA((devices,)),
            pltpu.SemaphoreType.DMA((devices,)),
            pltpu.SemaphoreType.DMA((blks,)),
            pltpu.SemaphoreType.DMA((blks,)),
        ],
        compiler_params=pltpu.CompilerParams(
            vmem_limit_bytes=VMEM_LIMIT, collective_id=0, has_side_effects=True),
        name="spread",
    )(own_rows, faces.reshape(half, slots), conductance)

    first = jnp.reshape(blk * lat_rows, (1,)).astype(jnp.int32)

    def full(*shape):
        return pl.BlockSpec(shape, lambda g: (0,) * len(shape))

    added, share = pl.pallas_call(
        functools.partial(grid_kernel, lons.bit_length() - 1),
        grid=(1,),
        in_specs=[smem(), full(devices, 2, slots), full(lats, lons), full(1, slots)],
        out_specs=[full(1, slots), full(lat_rows, lons)],
        out_shape=[jax.ShapeDtypeStruct((1, slots), F32), jax.ShapeDtypeStruct(conductance.shape, F32)],
        scratch_shapes=[pltpu.VMEM((lats, lons), F32)],
        compiler_params=params(),
        cost_estimate=pl.CostEstimate(flops=5 * 10**9, bytes_accessed=10**6, transcendentals=0),
        name="ionosphere",
    )(first, parts, conduct, own_rows)
    u = step(last_step_kernel, 0, u_a, halo_a, block(0), whole, (added, u), (full(1, slots), anywhere), {8: 0})
    return (u, share)


def solution(mesh):
    placed = (
        P(None, None, None, None, ("grp", "blk")),
        P(("grp", "blk")),
        P(None, ("grp", "blk")),
        P(("grp", "blk")),
        P(),
        P("blk", None),
    )
    return jax.shard_map(
        on_device,
        mesh=mesh,
        in_specs=placed,
        out_specs=(P(None, None, None, None, ("grp", "blk")), P("blk", None)),
        check_vma=False,
    )
```

```python
import functools

import jax
import jax.numpy as jnp
from jax import lax
from jax.experimental import pallas as pl
from jax.experimental.pallas import tpu as pltpu
from jax.sharding import PartitionSpec as P

ITERS = 3
EDGE = 128
FAR = 1 << 29
PAIR = 2
VMEM_LIMIT = 48 * 1024 * 1024
BF16 = jnp.bfloat16
F32 = jnp.float32


def params():
    return pltpu.CompilerParams(vmem_limit_bytes=VMEM_LIMIT)


def split(x):
    high = x.astype(BF16)
    low = (x - high.astype(F32)).astype(BF16)
    return jnp.concatenate([high, low], axis=0)


def picked(table, selector):
    rows = table.shape[0]
    both = jnp.dot(split(table), selector, preferred_element_type=F32)
    return both[:rows] + both[rows:]


def plane(ref, face):
    end = 0 if face % 2 == 0 else ref.shape[1] - 1
    if face < 2:
        return ref[:, end]
    if face < 4:
        return ref[:, :, end]
    return ref[:, :, :, end, :]


def one_hot(index, depth):
    rows = lax.broadcasted_iota(jnp.int32, (depth, index.shape[-1]), 0)
    return jnp.where(rows == index, 1.0, 0.0).astype(BF16)


def write_edges(ref, count, head_ref, tail_ref):
    size, slots = ref.shape[1], ref.shape[-1]
    lane = lax.broadcasted_iota(jnp.int32, (1, EDGE), 1)
    late = lane + (slots - EDGE) < count
    at = 0
    for face in range(6):
        cells = plane(ref, face)
        if face >= 2:
            cells = cells[:, 1 : size - 1]
        tiles = cells.shape[1]
        head_ref[:, at : at + tiles] = cells[..., :EDGE]
        tail_ref[:, at : at + tiles] = jnp.where(
            late, cells[..., slots - EDGE :], cells[..., slots - 2 * EDGE : slots - EDGE]
        )
        at += tiles


def read_edges(ref, face):
    size = ref.shape[2]
    end = 0 if face % 2 == 0 else size - 1
    if face < 2:
        return ref[:, face * size : (face + 1) * size]
    at = 2 * size + (face - 2) * (size - 2)
    middle = ref[:, at : at + size - 2]
    if face < 4:
        first, last = ref[:, end : end + 1], ref[:, size + end : size + end + 1]
    else:
        first = ref[:, 0:size, end, :][:, None]
        last = ref[:, size : 2 * size, end, :][:, None]
    return jnp.concatenate([first, middle, last], axis=1)


def edges_kernel(count_ref, u_ref, *refs):
    head_ref, tail_ref = refs[-2:]
    write_edges(u_ref, count_ref[0], head_ref, tail_ref)


def step_body(start, base_ref, count_ref, rates_ref, near_ref, lower_ref, upper_ref, u_ref, out_ref, selector, ghosts):
    pair, size, _, _, slots = u_ref.shape

    @pl.when(pl.program_id(0) == 0)
    def _():
        for face in range(6):
            index = near_ref[face : face + 1, :]
            index = jnp.where(index < 0, FAR, index - base_ref[0])
            index = jnp.where(
                index < 0,
                slots + (index & (EDGE - 1)),
                jnp.where(index >= slots, index + EDGE, index),
            )
            selector[face] = one_hot(index, slots + 2 * EDGE)

    own = [plane(u_ref, face) for face in range(6)]
    for face in range(6):
        rows = pair * size * size
        table = jnp.concatenate(
            [
                own[face ^ 1].reshape(rows, slots),
                read_edges(lower_ref, face ^ 1).reshape(rows, EDGE),
                read_edges(upper_ref, face ^ 1).reshape(rows, EDGE),
            ],
            axis=1,
        )
        taken = picked(table, selector[face]).reshape(pair, size, size, slots)
        outer = near_ref[face : face + 1, :] < 0
        ghosts[face] = jnp.where(outer, own[face], taken)

    row = lax.broadcasted_iota(jnp.int32, (size, slots), 0)
    first, last = row == 0, row == size - 1

    def variable(v, carry):
        live = lax.broadcasted_iota(jnp.int32, (1, slots), 1) < count_ref[0]
        factor = jnp.where(live, rates_ref[start + pl.program_id(0) * pair + v], 0.0)
        for i in range(size):
            for j in range(size):
                cell = u_ref[v, i, j]
                above = u_ref[v, i + 1, j] if i < size - 1 else ghosts[1, v, j]
                below = u_ref[v, i - 1, j] if i > 0 else ghosts[0, v, j]
                right = u_ref[v, i, j + 1] if j < size - 1 else ghosts[3, v, i]
                left = u_ref[v, i, j - 1] if j > 0 else ghosts[2, v, i]
                front = jnp.where(last, ghosts[5, v, i, j : j + 1, :], pltpu.roll(cell, size - 1, 0))
                back = jnp.where(first, ghosts[4, v, i, j : j + 1, :], pltpu.roll(cell, 1, 0))
                lap = ((above + below) + (right + left)) + ((front + back) - 6.0 * cell)
                out_ref[v, i, j] = cell + factor * lap
        return carry

    lax.fori_loop(0, pair, variable, 0)


def edge_step_kernel(start, base_ref, count_ref, rates_ref, near_ref, lower_ref, upper_ref, u_ref, *refs):
    out_ref, head_ref, tail_ref, selector, ghosts = refs[-5:]
    step_body(start, base_ref, count_ref, rates_ref, near_ref, lower_ref, upper_ref, u_ref, out_ref, selector, ghosts)
    write_edges(out_ref, count_ref[0], head_ref, tail_ref)


def sum_step_kernel(start, base_ref, count_ref, rates_ref, near_ref, lower_ref, upper_ref, u_ref, *refs):
    out_ref, sums_ref, selector, ghosts = refs[-4:]
    step_body(start, base_ref, count_ref, rates_ref, near_ref, lower_ref, upper_ref, u_ref, out_ref, selector, ghosts)
    for v in range(out_ref.shape[0]):
        sums_ref[0, v : v + 1, :] = jnp.sum(jnp.sum(out_ref[v, 0], axis=0), axis=0, keepdims=True)


def last_step_kernel(start, base_ref, count_ref, rates_ref, near_ref, lower_ref, upper_ref, u_ref, *refs):
    added_ref = refs[0]
    out_ref, selector, ghosts = refs[-3:]
    step_body(start, base_ref, count_ref, rates_ref, near_ref, lower_ref, upper_ref, u_ref, out_ref, selector, ghosts)

    @pl.when(pl.program_id(0) == 0)
    def _():
        out_ref[1, 0] = out_ref[1, 0] + added_ref[...]


def total(x):
    return jnp.sum(x, axis=(0, 1), keepdims=True)


def spread_kernel(groups, blks, rows_ref, faces_ref, cond_ref, parts_ref, whole_ref,
                  packet, landed, slabs, send_sem, recv_sem, slab_send_sem, slab_recv_sem):
    devices = groups * blks
    grp, blk = lax.axis_index("grp"), lax.axis_index("blk")
    me = grp * blks + blk

    def place(step):
        other = lax.rem(me + step, devices)
        return (other // blks, lax.rem(other, blks))

    def along(step):
        return (grp, lax.rem(blk + step, blks))

    barrier = pltpu.get_barrier_semaphore()

    def greet(step, carry):
        pl.semaphore_signal(barrier, inc=1, device_id=place(step), device_id_type=pl.DeviceIdType.MESH)
        return carry

    lax.fori_loop(1, devices, greet, 0)
    packet[0:1, :] = rows_ref[...].astype(F32)
    packet[1:2, :] = (faces_ref[2:3, :] - faces_ref[1:2, :]) / 8.0
    pl.semaphore_wait(barrier, devices - 1)

    def copy(step):
        return pltpu.make_async_remote_copy(
            src_ref=packet, dst_ref=landed.at[me], send_sem=send_sem.at[step], recv_sem=recv_sem.at[step],
            device_id=place(step), device_id_type=pl.DeviceIdType.MESH)

    def slab_copy(step):
        return pltpu.make_async_remote_copy(
            src_ref=cond_ref, dst_ref=slabs.at[blk], send_sem=slab_send_sem.at[step],
            recv_sem=slab_recv_sem.at[step], device_id=along(step), device_id_type=pl.DeviceIdType.MESH)

    def start(step, carry):
        copy(step).start()
        return carry

    def start_slab(step, carry):
        slab_copy(step).start()
        return carry

    def finish(step, carry):
        copy(step).wait()
        return carry

    def finish_slab(step, carry):
        slab_copy(step).wait()
        return carry

    lax.fori_loop(1, devices, start, 0)
    lax.fori_loop(1, blks, start_slab, 0)
    landed[me] = packet[...]
    slabs[blk] = cond_ref[...]
    lax.fori_loop(1, devices, finish, 0)
    lax.fori_loop(1, blks, finish_slab, 0)
    parts_ref[...] = landed[...]
    lats = cond_ref.shape[0]
    for b in range(blks):
        whole_ref[b * lats : (b + 1) * lats, :] = slabs[b]


def grid_kernel(shift, first_ref, parts_ref, cond_ref, rows_ref, added_ref, share_ref, held):
    lats, lons = cond_ref.shape
    devices, _, slots = parts_ref.shape
    mask = lons - 1

    def gathered(c, acc):
        for part in range(4):
            piece = parts_ref[c * 4 + part]
            cell = piece[0:1, :].astype(jnp.int32)
            current = piece[1:2, :]
            here = lax.broadcasted_iota(jnp.int32, (lats, slots), 0) == (cell >> shift)
            high = current.astype(BF16).astype(F32)
            low = current - high
            weighted = jnp.concatenate(
                [jnp.where(here, high, 0.0).astype(BF16), jnp.where(here, low, 0.0).astype(BF16)], axis=0
            )
            across = one_hot(cell & mask, lons)
            acc = acc + lax.dot_general(
                weighted, across, (((1,), (1,)), ((), ())), preferred_element_type=F32)
        return acc

    acc = lax.fori_loop(0, devices // 4, gathered, jnp.zeros((2 * lats, lons), F32))
    source = acc[:lats] + acc[lats:]

    weight = 4.0 + cond_ref[...]
    row = lax.broadcasted_iota(jnp.int32, (lats, lons), 0)
    potential = jnp.zeros_like(source)
    residual = source
    direction = source
    now = total(residual * residual)
    for _ in range(ITERS):
        south = jnp.where(row == 0, 0.0, pltpu.roll(direction, 1, 0))
        north = jnp.where(row == lats - 1, 0.0, pltpu.roll(direction, lats - 1, 0))
        beside = south + north + pltpu.roll(direction, 1, 1) + pltpu.roll(direction, lons - 1, 1)
        image = weight * direction - beside
        alpha = now / total(direction * image)
        potential = potential + alpha * direction
        residual = residual - alpha * image
        new = total(residual * residual)
        direction = residual + (new / now) * direction
        now = new

    held[...] = potential
    for r in range(share_ref.shape[0]):
        share_ref[r : r + 1, :] = held[pl.ds(first_ref[0] + r, 1), :]
    own = rows_ref[...]
    across = picked(potential, one_hot(jnp.where(own < 0, -1, own & mask), lons))
    here = lax.broadcasted_iota(jnp.int32, across.shape, 0) == (own >> shift)
    added_ref[...] = jnp.sum(jnp.where(here, across, 0.0), axis=0, keepdims=True)


def smem():
    return pl.BlockSpec(memory_space=pltpu.SMEM)


def on_device(state, counts, neighbours, rows, rates, conductance):
    vars_, size, _, _, slots = state.shape
    axes = ("grp", "blk")
    groups, blks = lax.axis_size("grp"), lax.axis_size("blk")
    devices = groups * blks
    blk = lax.axis_index("blk")
    device = lax.axis_index("grp") * blks + blk
    base = jnp.reshape(device * slots, (1,)).astype(jnp.int32)
    half = vars_ // 2
    grid = (half // PAIR,)
    tiles = 2 * size + 4 * (size - 2)
    edge = pl.BlockSpec((PAIR, tiles, size, EDGE), lambda g: (g, 0, 0, 0))
    near = pl.BlockSpec(neighbours.shape, lambda g: (0, 0))
    sums = pl.BlockSpec((1, PAIR, slots), lambda g: (g, 0, 0))
    anywhere = pl.BlockSpec(memory_space=pl.ANY)
    whole = jax.ShapeDtypeStruct(state.shape, F32)
    part = jax.ShapeDtypeStruct((half,) + state.shape[1:], F32)
    edge_shape = jax.ShapeDtypeStruct((half, tiles, size, EDGE), F32)
    sums_shape = jax.ShapeDtypeStruct((half // PAIR, PAIR, slots), F32)
    up = [(d, d + 1) for d in range(devices - 1)]
    down = [(d + 1, d) for d in range(devices - 1)]

    def block(start):
        return pl.BlockSpec((PAIR, size, size, size, slots), lambda g: (g + start // PAIR, 0, 0, 0, 0))

    def exchange(head, tail):
        return lax.ppermute(tail, axes, up), lax.ppermute(head, axes, down)

    def edges(start, *after):
        return pl.pallas_call(
            edges_kernel,
            grid=grid,
            in_specs=[smem(), block(start)] + [anywhere] * len(after),
            out_specs=[edge, edge],
            out_shape=[edge_shape, edge_shape],
            compiler_params=params(),
            cost_estimate=pl.CostEstimate(flops=10**6, bytes_accessed=8 * 10**6, transcendentals=0),
            name="edges",
        )(counts, state, *after)

    def step(kernel, start, u, halo, out_specs, out_shape, extra=(), extra_specs=(), aliases={}):
        return pl.pallas_call(
            functools.partial(kernel, start),
            grid=grid,
            in_specs=[smem(), smem(), smem(), near, edge, edge, block(start if u is state else 0)]
            + list(extra_specs),
            out_specs=out_specs,
            out_shape=out_shape,
            scratch_shapes=[
                pltpu.VMEM((6, slots + 2 * EDGE, slots), BF16),
                pltpu.VMEM((6, PAIR, size, size, slots), F32),
            ],
            input_output_aliases=aliases,
            compiler_params=params(),
            cost_estimate=pl.CostEstimate(flops=5 * 10**9, bytes_accessed=30 * 10**6, transcendentals=0),
            name="step",
        )(base, counts, rates, neighbours, *halo, u, *extra)

    head_b, tail_b = edges(half)
    halo_b = exchange(head_b, tail_b)
    head_a, tail_a = edges(0, head_b)
    head_a, tail_a, *halo_b = lax.optimization_barrier((head_a, tail_a, *halo_b))
    halo_a = exchange(head_a, tail_a)
    outs = [block(0), edge, edge]
    shapes = [part, edge_shape, edge_shape]
    u_b, head_b, tail_b = step(edge_step_kernel, half, state, halo_b, outs, shapes)
    halo_b = exchange(head_b, tail_b)
    u_a, head_a, tail_a = step(edge_step_kernel, 0, state, halo_a, outs, shapes, (head_b,), (anywhere,))
    halo_a = exchange(head_a, tail_a)
    u, faces = step(
        sum_step_kernel, half, u_b, halo_b, [block(half), sums], [whole, sums_shape], (head_a,), (anywhere,))

    lat_rows, lons = conductance.shape
    lats = lat_rows * blks
    own_rows = rows.reshape(1, slots)
    parts, conduct = pl.pallas_call(
        functools.partial(spread_kernel, groups, blks),
        in_specs=[pl.BlockSpec(memory_space=pltpu.VMEM)] * 3,
        out_specs=[pl.BlockSpec(memory_space=pltpu.VMEM)] * 2,
        out_shape=[jax.ShapeDtypeStruct((devices, 2, slots), F32), jax.ShapeDtypeStruct((lats, lons), F32)],
        scratch_shapes=[
            pltpu.VMEM((2, slots), F32),
            pltpu.VMEM((devices, 2, slots), F32),
            pltpu.VMEM((blks, lat_rows, lons), F32),
            pltpu.SemaphoreType.DMA((devices,)),
            pltpu.SemaphoreType.DMA((devices,)),
            pltpu.SemaphoreType.DMA((blks,)),
            pltpu.SemaphoreType.DMA((blks,)),
        ],
        compiler_params=pltpu.CompilerParams(
            vmem_limit_bytes=VMEM_LIMIT, collective_id=0, has_side_effects=True),
        name="spread",
    )(own_rows, faces.reshape(half, slots), conductance)

    first = jnp.reshape(blk * lat_rows, (1,)).astype(jnp.int32)

    def full(*shape):
        return pl.BlockSpec(shape, lambda g: (0,) * len(shape))

    added, share = pl.pallas_call(
        functools.partial(grid_kernel, lons.bit_length() - 1),
        grid=(1,),
        in_specs=[smem(), full(devices, 2, slots), full(lats, lons), full(1, slots)],
        out_specs=[full(1, slots), full(lat_rows, lons)],
        out_shape=[jax.ShapeDtypeStruct((1, slots), F32), jax.ShapeDtypeStruct(conductance.shape, F32)],
        scratch_shapes=[pltpu.VMEM((lats, lons), F32)],
        compiler_params=params(),
        cost_estimate=pl.CostEstimate(flops=5 * 10**9, bytes_accessed=10**6, transcendentals=0),
        name="ionosphere",
    )(first, parts, conduct, own_rows)
    u = step(last_step_kernel, 0, u_a, halo_a, block(0), whole, (added, u), (full(1, slots), anywhere), {8: 0})
    return (u, share)


def solution(mesh):
    placed = (
        P(None, None, None, None, ("grp", "blk")),
        P(("grp", "blk")),
        P(None, ("grp", "blk")),
        P(("grp", "blk")),
        P(),
        P("blk", None),
    )
    return jax.shard_map(
        on_device,
        mesh=mesh,
        in_specs=placed,
        out_specs=(P(None, None, None, None, ("grp", "blk")), P("blk", None)),
        check_vma=False,
    )
```

```python
import functools

import jax
import jax.numpy as jnp
from jax import lax
from jax.experimental import pallas as pl
from jax.experimental.pallas import tpu as pltpu
from jax.sharding import PartitionSpec as P

ITERS = 3
EDGE = 128
FAR = 1 << 29
PAIR = 2
VMEM_LIMIT = 48 * 1024 * 1024
BF16 = jnp.bfloat16
F32 = jnp.float32


def params():
    return pltpu.CompilerParams(vmem_limit_bytes=VMEM_LIMIT)


def split(x):
    high = x.astype(BF16)
    low = (x - high.astype(F32)).astype(BF16)
    return jnp.concatenate([high, low], axis=0)


def picked(table, selector):
    rows = table.shape[0]
    both = jnp.dot(split(table), selector, preferred_element_type=F32)
    return both[:rows] + both[rows:]


def plane(ref, face):
    end = 0 if face % 2 == 0 else ref.shape[1] - 1
    if face < 2:
        return ref[:, end]
    if face < 4:
        return ref[:, :, end]
    return ref[:, :, :, end, :]


def one_hot(index, depth):
    rows = lax.broadcasted_iota(jnp.int32, (depth, index.shape[-1]), 0)
    return jnp.where(rows == index, 1.0, 0.0).astype(BF16)


def write_edges(ref, count, head_ref, tail_ref):
    size, slots = ref.shape[1], ref.shape[-1]
    lane = lax.broadcasted_iota(jnp.int32, (1, EDGE), 1)
    late = lane + (slots - EDGE) < count
    at = 0
    for face in range(6):
        cells = plane(ref, face)
        if face >= 2:
            cells = cells[:, 1 : size - 1]
        tiles = cells.shape[1]
        head_ref[:, at : at + tiles] = cells[..., :EDGE]
        tail_ref[:, at : at + tiles] = jnp.where(
            late, cells[..., slots - EDGE :], cells[..., slots - 2 * EDGE : slots - EDGE]
        )
        at += tiles


def read_edges(ref, face):
    size = ref.shape[2]
    end = 0 if face % 2 == 0 else size - 1
    if face < 2:
        return ref[:, face * size : (face + 1) * size]
    at = 2 * size + (face - 2) * (size - 2)
    middle = ref[:, at : at + size - 2]
    if face < 4:
        first, last = ref[:, end : end + 1], ref[:, size + end : size + end + 1]
    else:
        first = ref[:, 0:size, end, :][:, None]
        last = ref[:, size : 2 * size, end, :][:, None]
    return jnp.concatenate([first, middle, last], axis=1)


def edges_kernel(count_ref, u_ref, *refs):
    head_ref, tail_ref = refs[-2:]
    write_edges(u_ref, count_ref[0], head_ref, tail_ref)


def step_body(start, base_ref, count_ref, rates_ref, near_ref, lower_ref, upper_ref, u_ref, out_ref, selector, ghosts):
    pair, size, _, _, slots = u_ref.shape

    @pl.when(pl.program_id(0) == 0)
    def _():
        for face in range(6):
            index = near_ref[face : face + 1, :]
            index = jnp.where(index < 0, FAR, index - base_ref[0])
            index = jnp.where(
                index < 0,
                slots + (index & (EDGE - 1)),
                jnp.where(index >= slots, index + EDGE, index),
            )
            selector[face] = one_hot(index, selector.shape[1])

    own = [plane(u_ref, face) for face in range(6)]
    for face in range(6):
        rows = pair * size * size
        table = own[face ^ 1].reshape(rows, slots)
        if lower_ref is not None:
            table = jnp.concatenate(
                [
                    table,
                    read_edges(lower_ref, face ^ 1).reshape(rows, EDGE),
                    read_edges(upper_ref, face ^ 1).reshape(rows, EDGE),
                ],
                axis=1,
            )
        taken = picked(table, selector[face]).reshape(pair, size, size, slots)
        outer = near_ref[face : face + 1, :] < 0
        ghosts[face] = jnp.where(outer, own[face], taken)

    row = lax.broadcasted_iota(jnp.int32, (size, slots), 0)
    first, last = row == 0, row == size - 1

    def variable(v, carry):
        live = lax.broadcasted_iota(jnp.int32, (1, slots), 1) < count_ref[0]
        factor = jnp.where(live, rates_ref[start + pl.program_id(0) * pair + v], 0.0)
        for i in range(size):
            for j in range(size):
                cell = u_ref[v, i, j]
                above = u_ref[v, i + 1, j] if i < size - 1 else ghosts[1, v, j]
                below = u_ref[v, i - 1, j] if i > 0 else ghosts[0, v, j]
                right = u_ref[v, i, j + 1] if j < size - 1 else ghosts[3, v, i]
                left = u_ref[v, i, j - 1] if j > 0 else ghosts[2, v, i]
                front = jnp.where(last, ghosts[5, v, i, j : j + 1, :], pltpu.roll(cell, size - 1, 0))
                back = jnp.where(first, ghosts[4, v, i, j : j + 1, :], pltpu.roll(cell, 1, 0))
                lap = ((above + below) + (right + left)) + ((front + back) - 6.0 * cell)
                out_ref[v, i, j] = cell + factor * lap
        return carry

    lax.fori_loop(0, pair, variable, 0)


def edge_step_kernel(start, base_ref, count_ref, rates_ref, near_ref, lower_ref, upper_ref, u_ref, *refs):
    out_ref, head_ref, tail_ref, selector, ghosts = refs[-5:]
    step_body(start, base_ref, count_ref, rates_ref, near_ref, lower_ref, upper_ref, u_ref, out_ref, selector, ghosts)
    write_edges(out_ref, count_ref[0], head_ref, tail_ref)


def local_step_kernel(start, base_ref, count_ref, rates_ref, near_ref, u_ref, out_ref, selector, ghosts):
    step_body(start, base_ref, count_ref, rates_ref, near_ref, None, None, u_ref, out_ref, selector, ghosts)


def remote_step_kernel(start, base_ref, count_ref, rates_ref, near_ref, lower_ref, upper_ref, u_ref,
                       out_ref, head_ref, tail_ref, selector, ghosts):
    pair, size, _, _, slots = u_ref.shape

    @pl.when(pl.program_id(0) == 0)
    def _():
        for face in range(6):
            index = near_ref[face : face + 1, :]
            index = jnp.where(index < 0, FAR, index - base_ref[0])
            beyond = jnp.where(index >= slots, index - slots + EDGE, -1)
            index = jnp.where(index < 0, index & (EDGE - 1), beyond)
            selector[face] = one_hot(index, 2 * EDGE)

    for face in range(6):
        rows = pair * size * size
        table = jnp.concatenate(
            [
                read_edges(lower_ref, face ^ 1).reshape(rows, EDGE),
                read_edges(upper_ref, face ^ 1).reshape(rows, EDGE),
            ],
            axis=1,
        )
        ghosts[face] = picked(table, selector[face]).reshape(pair, size, size, slots)

    row = lax.broadcasted_iota(jnp.int32, (size, slots), 0)
    first, last = row == 0, row == size - 1

    def variable(v, carry):
        live = lax.broadcasted_iota(jnp.int32, (1, slots), 1) < count_ref[0]
        factor = jnp.where(live, rates_ref[start + pl.program_id(0) * pair + v], 0.0)
        for i in range(size):
            for j in range(size):
                extra = jnp.where(first, ghosts[4, v, i, j : j + 1, :], 0.0)
                extra = jnp.where(last, ghosts[5, v, i, j : j + 1, :], extra)
                if i == 0:
                    extra = extra + ghosts[0, v, j]
                if i == size - 1:
                    extra = extra + ghosts[1, v, j]
                if j == 0:
                    extra = extra + ghosts[2, v, i]
                if j == size - 1:
                    extra = extra + ghosts[3, v, i]
                out_ref[v, i, j] = u_ref[v, i, j] + factor * extra
        return carry

    lax.fori_loop(0, pair, variable, 0)
    write_edges(out_ref, count_ref[0], head_ref, tail_ref)


def sum_step_kernel(start, base_ref, count_ref, rates_ref, near_ref, lower_ref, upper_ref, u_ref, *refs):
    out_ref, sums_ref, selector, ghosts = refs[-4:]
    step_body(start, base_ref, count_ref, rates_ref, near_ref, lower_ref, upper_ref, u_ref, out_ref, selector, ghosts)
    for v in range(out_ref.shape[0]):
        sums_ref[0, v : v + 1, :] = jnp.sum(jnp.sum(out_ref[v, 0], axis=0), axis=0, keepdims=True)


def last_step_kernel(start, base_ref, count_ref, rates_ref, near_ref, lower_ref, upper_ref, u_ref, *refs):
    added_ref = refs[0]
    out_ref, selector, ghosts = refs[-3:]
    step_body(start, base_ref, count_ref, rates_ref, near_ref, lower_ref, upper_ref, u_ref, out_ref, selector, ghosts)

    @pl.when(pl.program_id(0) == 0)
    def _():
        out_ref[1, 0] = out_ref[1, 0] + added_ref[...]


def total(x):
    return jnp.sum(x, axis=(0, 1), keepdims=True)


def spread_kernel(groups, blks, rows_ref, faces_ref, cond_ref, parts_ref, whole_ref,
                  packet, landed, slabs, send_sem, recv_sem, slab_send_sem, slab_recv_sem):
    devices = groups * blks
    grp, blk = lax.axis_index("grp"), lax.axis_index("blk")
    me = grp * blks + blk

    def place(step):
        other = lax.rem(me + step, devices)
        return (other // blks, lax.rem(other, blks))

    def along(step):
        return (grp, lax.rem(blk + step, blks))

    barrier = pltpu.get_barrier_semaphore()

    def greet(step, carry):
        pl.semaphore_signal(barrier, inc=1, device_id=place(step), device_id_type=pl.DeviceIdType.MESH)
        return carry

    lax.fori_loop(1, devices, greet, 0)
    packet[0:1, :] = rows_ref[...].astype(F32)
    packet[1:2, :] = (faces_ref[2:3, :] - faces_ref[1:2, :]) / 8.0
    pl.semaphore_wait(barrier, devices - 1)

    def copy(step):
        return pltpu.make_async_remote_copy(
            src_ref=packet, dst_ref=landed.at[me], send_sem=send_sem.at[step], recv_sem=recv_sem.at[step],
            device_id=place(step), device_id_type=pl.DeviceIdType.MESH)

    def slab_copy(step):
        return pltpu.make_async_remote_copy(
            src_ref=cond_ref, dst_ref=slabs.at[blk], send_sem=slab_send_sem.at[step],
            recv_sem=slab_recv_sem.at[step], device_id=along(step), device_id_type=pl.DeviceIdType.MESH)

    def start(step, carry):
        copy(step).start()
        return carry

    def start_slab(step, carry):
        slab_copy(step).start()
        return carry

    def finish(step, carry):
        copy(step).wait()
        return carry

    def finish_slab(step, carry):
        slab_copy(step).wait()
        return carry

    lax.fori_loop(1, devices, start, 0)
    lax.fori_loop(1, blks, start_slab, 0)
    landed[me] = packet[...]
    slabs[blk] = cond_ref[...]
    lax.fori_loop(1, devices, finish, 0)
    lax.fori_loop(1, blks, finish_slab, 0)
    parts_ref[...] = landed[...]
    lats = cond_ref.shape[0]
    for b in range(blks):
        whole_ref[b * lats : (b + 1) * lats, :] = slabs[b]


def grid_kernel(shift, first_ref, parts_ref, cond_ref, rows_ref, added_ref, share_ref, held):
    lats, lons = cond_ref.shape
    devices, _, slots = parts_ref.shape
    mask = lons - 1

    def gathered(c, acc):
        for part in range(4):
            piece = parts_ref[c * 4 + part]
            cell = piece[0:1, :].astype(jnp.int32)
            current = piece[1:2, :]
            here = lax.broadcasted_iota(jnp.int32, (lats, slots), 0) == (cell >> shift)
            high = current.astype(BF16).astype(F32)
            low = current - high
            weighted = jnp.concatenate(
                [jnp.where(here, high, 0.0).astype(BF16), jnp.where(here, low, 0.0).astype(BF16)], axis=0
            )
            across = one_hot(cell & mask, lons)
            acc = acc + lax.dot_general(
                weighted, across, (((1,), (1,)), ((), ())), preferred_element_type=F32)
        return acc

    acc = lax.fori_loop(0, devices // 4, gathered, jnp.zeros((2 * lats, lons), F32))
    source = acc[:lats] + acc[lats:]

    weight = 4.0 + cond_ref[...]
    row = lax.broadcasted_iota(jnp.int32, (lats, lons), 0)
    potential = jnp.zeros_like(source)
    residual = source
    direction = source
    now = total(residual * residual)
    for _ in range(ITERS):
        south = jnp.where(row == 0, 0.0, pltpu.roll(direction, 1, 0))
        north = jnp.where(row == lats - 1, 0.0, pltpu.roll(direction, lats - 1, 0))
        beside = south + north + pltpu.roll(direction, 1, 1) + pltpu.roll(direction, lons - 1, 1)
        image = weight * direction - beside
        alpha = now / total(direction * image)
        potential = potential + alpha * direction
        residual = residual - alpha * image
        new = total(residual * residual)
        direction = residual + (new / now) * direction
        now = new

    held[...] = potential
    for r in range(share_ref.shape[0]):
        share_ref[r : r + 1, :] = held[pl.ds(first_ref[0] + r, 1), :]
    own = rows_ref[...]
    across = picked(potential, one_hot(jnp.where(own < 0, -1, own & mask), lons))
    here = lax.broadcasted_iota(jnp.int32, across.shape, 0) == (own >> shift)
    added_ref[...] = jnp.sum(jnp.where(here, across, 0.0), axis=0, keepdims=True)


def smem():
    return pl.BlockSpec(memory_space=pltpu.SMEM)


def on_device(state, counts, neighbours, rows, rates, conductance):
    vars_, size, _, _, slots = state.shape
    axes = ("grp", "blk")
    groups, blks = lax.axis_size("grp"), lax.axis_size("blk")
    devices = groups * blks
    blk = lax.axis_index("blk")
    device = lax.axis_index("grp") * blks + blk
    base = jnp.reshape(device * slots, (1,)).astype(jnp.int32)
    half = vars_ // 2
    grid = (half // PAIR,)
    tiles = 2 * size + 4 * (size - 2)
    edge = pl.BlockSpec((PAIR, tiles, size, EDGE), lambda g: (g, 0, 0, 0))
    near = pl.BlockSpec(neighbours.shape, lambda g: (0, 0))
    sums = pl.BlockSpec((1, PAIR, slots), lambda g: (g, 0, 0))
    anywhere = pl.BlockSpec(memory_space=pl.ANY)
    whole = jax.ShapeDtypeStruct(state.shape, F32)
    part = jax.ShapeDtypeStruct((half,) + state.shape[1:], F32)
    edge_shape = jax.ShapeDtypeStruct((half, tiles, size, EDGE), F32)
    sums_shape = jax.ShapeDtypeStruct((half // PAIR, PAIR, slots), F32)
    up = [(d, d + 1) for d in range(devices - 1)]
    down = [(d + 1, d) for d in range(devices - 1)]

    def block(start):
        return pl.BlockSpec((PAIR, size, size, size, slots), lambda g: (g + start // PAIR, 0, 0, 0, 0))

    def exchange(head, tail):
        return lax.ppermute(tail, axes, up), lax.ppermute(head, axes, down)

    def edges(start, *after):
        return pl.pallas_call(
            edges_kernel,
            grid=grid,
            in_specs=[smem(), block(start)] + [anywhere] * len(after),
            out_specs=[edge, edge],
            out_shape=[edge_shape, edge_shape],
            compiler_params=params(),
            cost_estimate=pl.CostEstimate(flops=10**6, bytes_accessed=8 * 10**6, transcendentals=0),
            name="edges",
        )(counts, state, *after)

    def step(kernel, start, u, halo, out_specs, out_shape, extra=(), extra_specs=(), aliases={}, depth=slots + 2 * EDGE):
        return pl.pallas_call(
            functools.partial(kernel, start),
            grid=grid,
            in_specs=[smem(), smem(), smem(), near]
            + [edge] * len(halo)
            + [block(start if u is state else 0)]
            + list(extra_specs),
            out_specs=out_specs,
            out_shape=out_shape,
            scratch_shapes=[
                pltpu.VMEM((6, depth, slots), BF16),
                pltpu.VMEM((6, PAIR, size, size, slots), F32),
            ],
            input_output_aliases=aliases,
            compiler_params=params(),
            cost_estimate=pl.CostEstimate(flops=5 * 10**9, bytes_accessed=30 * 10**6, transcendentals=0),
            name="step",
        )(base, counts, rates, neighbours, *halo, u, *extra)

    head_b, tail_b = edges(half)
    halo_b = exchange(head_b, tail_b)
    u_b = step(local_step_kernel, half, state, (), block(0), part, depth=slots)
    head_a, tail_a = edges(0, u_b)
    head_a, tail_a, *halo_b = lax.optimization_barrier((head_a, tail_a, *halo_b))
    halo_a = exchange(head_a, tail_a)
    outs = [block(0), edge, edge]
    shapes = [part, edge_shape, edge_shape]
    u_b, head_b, tail_b = step(remote_step_kernel, half, u_b, halo_b, outs, shapes, depth=2 * EDGE)
    halo_b = exchange(head_b, tail_b)
    u_a, head_a, tail_a = step(edge_step_kernel, 0, state, halo_a, outs, shapes, (head_b,), (anywhere,))
    halo_a = exchange(head_a, tail_a)
    u, faces = step(
        sum_step_kernel, half, u_b, halo_b, [block(half), sums], [whole, sums_shape], (head_a,), (anywhere,))

    lat_rows, lons = conductance.shape
    lats = lat_rows * blks
    own_rows = rows.reshape(1, slots)
    parts, conduct = pl.pallas_call(
        functools.partial(spread_kernel, groups, blks),
        in_specs=[pl.BlockSpec(memory_space=pltpu.VMEM)] * 3,
        out_specs=[pl.BlockSpec(memory_space=pltpu.VMEM)] * 2,
        out_shape=[jax.ShapeDtypeStruct((devices, 2, slots), F32), jax.ShapeDtypeStruct((lats, lons), F32)],
        scratch_shapes=[
            pltpu.VMEM((2, slots), F32),
            pltpu.VMEM((devices, 2, slots), F32),
            pltpu.VMEM((blks, lat_rows, lons), F32),
            pltpu.SemaphoreType.DMA((devices,)),
            pltpu.SemaphoreType.DMA((devices,)),
            pltpu.SemaphoreType.DMA((blks,)),
            pltpu.SemaphoreType.DMA((blks,)),
        ],
        compiler_params=pltpu.CompilerParams(
            vmem_limit_bytes=VMEM_LIMIT, collective_id=0, has_side_effects=True),
        name="spread",
    )(own_rows, faces.reshape(half, slots), conductance)

    first = jnp.reshape(blk * lat_rows, (1,)).astype(jnp.int32)

    def full(*shape):
        return pl.BlockSpec(shape, lambda g: (0,) * len(shape))

    added, share = pl.pallas_call(
        functools.partial(grid_kernel, lons.bit_length() - 1),
        grid=(1,),
        in_specs=[smem(), full(devices, 2, slots), full(lats, lons), full(1, slots)],
        out_specs=[full(1, slots), full(lat_rows, lons)],
        out_shape=[jax.ShapeDtypeStruct((1, slots), F32), jax.ShapeDtypeStruct(conductance.shape, F32)],
        scratch_shapes=[pltpu.VMEM((lats, lons), F32)],
        compiler_params=params(),
        cost_estimate=pl.CostEstimate(flops=5 * 10**9, bytes_accessed=10**6, transcendentals=0),
        name="ionosphere",
    )(first, parts, conduct, own_rows)
    u = step(last_step_kernel, 0, u_a, halo_a, block(0), whole, (added, u), (full(1, slots), anywhere), {8: 0})
    return (u, share)


def solution(mesh):
    placed = (
        P(None, None, None, None, ("grp", "blk")),
        P(("grp", "blk")),
        P(None, ("grp", "blk")),
        P(("grp", "blk")),
        P(),
        P("blk", None),
    )
    return jax.shard_map(
        on_device,
        mesh=mesh,
        in_specs=placed,
        out_specs=(P(None, None, None, None, ("grp", "blk")), P("blk", None)),
        check_vma=False,
    )
```

```python
import functools

import jax
import jax.numpy as jnp
from jax import lax
from jax.experimental import pallas as pl
from jax.experimental.pallas import tpu as pltpu
from jax.sharding import PartitionSpec as P

ITERS = 3
EDGE = 128
FAR = 1 << 29
PAIR = 4
VMEM_LIMIT = 48 * 1024 * 1024
BF16 = jnp.bfloat16
F32 = jnp.float32


def params():
    return pltpu.CompilerParams(vmem_limit_bytes=VMEM_LIMIT)


def split(x):
    high = x.astype(BF16)
    low = (x - high.astype(F32)).astype(BF16)
    return jnp.concatenate([high, low], axis=0)


def picked(table, selector):
    rows = table.shape[0]
    both = jnp.dot(split(table), selector, preferred_element_type=F32)
    return both[:rows] + both[rows:]


def plane(ref, face):
    end = 0 if face % 2 == 0 else ref.shape[1] - 1
    if face < 2:
        return ref[:, end]
    if face < 4:
        return ref[:, :, end]
    return ref[:, :, :, end, :]


def one_hot(index, depth):
    rows = lax.broadcasted_iota(jnp.int32, (depth, index.shape[-1]), 0)
    return jnp.where(rows == index, 1.0, 0.0).astype(BF16)


def write_edges(ref, count, head_ref, tail_ref):
    size, slots = ref.shape[1], ref.shape[-1]
    lane = lax.broadcasted_iota(jnp.int32, (1, EDGE), 1)
    late = lane + (slots - EDGE) < count
    at = 0
    for face in range(6):
        cells = plane(ref, face)
        if face >= 2:
            cells = cells[:, 1 : size - 1]
        tiles = cells.shape[1]
        head_ref[:, at : at + tiles] = cells[..., :EDGE]
        tail_ref[:, at : at + tiles] = jnp.where(
            late, cells[..., slots - EDGE :], cells[..., slots - 2 * EDGE : slots - EDGE]
        )
        at += tiles


def read_edges(ref, face):
    size = ref.shape[2]
    end = 0 if face % 2 == 0 else size - 1
    if face < 2:
        return ref[:, face * size : (face + 1) * size]
    at = 2 * size + (face - 2) * (size - 2)
    middle = ref[:, at : at + size - 2]
    if face < 4:
        first, last = ref[:, end : end + 1], ref[:, size + end : size + end + 1]
    else:
        first = ref[:, 0:size, end, :][:, None]
        last = ref[:, size : 2 * size, end, :][:, None]
    return jnp.concatenate([first, middle, last], axis=1)


def edges_kernel(count_ref, u_ref, *refs):
    head_ref, tail_ref = refs[-2:]
    write_edges(u_ref, count_ref[0], head_ref, tail_ref)


def step_body(start, base_ref, count_ref, rates_ref, near_ref, lower_ref, upper_ref, u_ref, out_ref, selector, ghosts):
    pair, size, _, _, slots = u_ref.shape

    @pl.when(pl.program_id(0) == 0)
    def _():
        for face in range(6):
            index = near_ref[face : face + 1, :]
            index = jnp.where(index < 0, FAR, index - base_ref[0])
            index = jnp.where(
                index < 0,
                slots + (index & (EDGE - 1)),
                jnp.where(index >= slots, index + EDGE, index),
            )
            selector[face] = one_hot(index, slots + 2 * EDGE)

    own = [plane(u_ref, face) for face in range(6)]
    for face in range(6):
        rows = pair * size * size
        table = jnp.concatenate(
            [
                own[face ^ 1].reshape(rows, slots),
                read_edges(lower_ref, face ^ 1).reshape(rows, EDGE),
                read_edges(upper_ref, face ^ 1).reshape(rows, EDGE),
            ],
            axis=1,
        )
        taken = picked(table, selector[face]).reshape(pair, size, size, slots)
        outer = near_ref[face : face + 1, :] < 0
        ghosts[face] = jnp.where(outer, own[face], taken)

    row = lax.broadcasted_iota(jnp.int32, (size, slots), 0)
    first, last = row == 0, row == size - 1

    def variable(v, carry):
        live = lax.broadcasted_iota(jnp.int32, (1, slots), 1) < count_ref[0]
        factor = jnp.where(live, rates_ref[start + pl.program_id(0) * pair + v], 0.0)
        for i in range(size):
            for j in range(size):
                cell = u_ref[v, i, j]
                above = u_ref[v, i + 1, j] if i < size - 1 else ghosts[1, v, j]
                below = u_ref[v, i - 1, j] if i > 0 else ghosts[0, v, j]
                right = u_ref[v, i, j + 1] if j < size - 1 else ghosts[3, v, i]
                left = u_ref[v, i, j - 1] if j > 0 else ghosts[2, v, i]
                front = jnp.where(last, ghosts[5, v, i, j : j + 1, :], pltpu.roll(cell, size - 1, 0))
                back = jnp.where(first, ghosts[4, v, i, j : j + 1, :], pltpu.roll(cell, 1, 0))
                lap = ((above + below) + (right + left)) + ((front + back) - 6.0 * cell)
                out_ref[v, i, j] = cell + factor * lap
        return carry

    lax.fori_loop(0, pair, variable, 0)


def edge_step_kernel(start, base_ref, count_ref, rates_ref, near_ref, lower_ref, upper_ref, u_ref, *refs):
    out_ref, head_ref, tail_ref, selector, ghosts = refs[-5:]
    step_body(start, base_ref, count_ref, rates_ref, near_ref, lower_ref, upper_ref, u_ref, out_ref, selector, ghosts)
    write_edges(out_ref, count_ref[0], head_ref, tail_ref)


def sum_step_kernel(start, base_ref, count_ref, rates_ref, near_ref, lower_ref, upper_ref, u_ref, *refs):
    out_ref, sums_ref, selector, ghosts = refs[-4:]
    step_body(start, base_ref, count_ref, rates_ref, near_ref, lower_ref, upper_ref, u_ref, out_ref, selector, ghosts)
    for v in range(out_ref.shape[0]):
        sums_ref[0, v : v + 1, :] = jnp.sum(jnp.sum(out_ref[v, 0], axis=0), axis=0, keepdims=True)


def last_step_kernel(start, base_ref, count_ref, rates_ref, near_ref, lower_ref, upper_ref, u_ref, *refs):
    added_ref = refs[0]
    out_ref, selector, ghosts = refs[-3:]
    step_body(start, base_ref, count_ref, rates_ref, near_ref, lower_ref, upper_ref, u_ref, out_ref, selector, ghosts)

    @pl.when(pl.program_id(0) == 0)
    def _():
        out_ref[1, 0] = out_ref[1, 0] + added_ref[...]


def total(x):
    return jnp.sum(x, axis=(0, 1), keepdims=True)


def spread_kernel(groups, blks, rows_ref, faces_ref, cond_ref, parts_ref, whole_ref,
                  packet, landed, slabs, send_sem, recv_sem, slab_send_sem, slab_recv_sem):
    devices = groups * blks
    grp, blk = lax.axis_index("grp"), lax.axis_index("blk")
    me = grp * blks + blk

    def place(step):
        other = lax.rem(me + step, devices)
        return (other // blks, lax.rem(other, blks))

    def along(step):
        return (grp, lax.rem(blk + step, blks))

    barrier = pltpu.get_barrier_semaphore()

    def greet(step, carry):
        pl.semaphore_signal(barrier, inc=1, device_id=place(step), device_id_type=pl.DeviceIdType.MESH)
        return carry

    lax.fori_loop(1, devices, greet, 0)
    packet[0:1, :] = rows_ref[...].astype(F32)
    packet[1:2, :] = (faces_ref[2:3, :] - faces_ref[1:2, :]) / 8.0
    pl.semaphore_wait(barrier, devices - 1)

    def copy(step):
        return pltpu.make_async_remote_copy(
            src_ref=packet, dst_ref=landed.at[me], send_sem=send_sem.at[step], recv_sem=recv_sem.at[step],
            device_id=place(step), device_id_type=pl.DeviceIdType.MESH)

    def slab_copy(step):
        return pltpu.make_async_remote_copy(
            src_ref=cond_ref, dst_ref=slabs.at[blk], send_sem=slab_send_sem.at[step],
            recv_sem=slab_recv_sem.at[step], device_id=along(step), device_id_type=pl.DeviceIdType.MESH)

    def start(step, carry):
        copy(step).start()
        return carry

    def start_slab(step, carry):
        slab_copy(step).start()
        return carry

    def finish(step, carry):
        copy(step).wait()
        return carry

    def finish_slab(step, carry):
        slab_copy(step).wait()
        return carry

    lax.fori_loop(1, devices, start, 0)
    lax.fori_loop(1, blks, start_slab, 0)
    landed[me] = packet[...]
    slabs[blk] = cond_ref[...]
    lax.fori_loop(1, devices, finish, 0)
    lax.fori_loop(1, blks, finish_slab, 0)
    parts_ref[...] = landed[...]
    lats = cond_ref.shape[0]
    for b in range(blks):
        whole_ref[b * lats : (b + 1) * lats, :] = slabs[b]


def grid_kernel(shift, first_ref, parts_ref, cond_ref, rows_ref, added_ref, share_ref, held):
    lats, lons = cond_ref.shape
    devices, _, slots = parts_ref.shape
    mask = lons - 1

    def gathered(c, acc):
        for part in range(4):
            piece = parts_ref[c * 4 + part]
            cell = piece[0:1, :].astype(jnp.int32)
            current = piece[1:2, :]
            here = lax.broadcasted_iota(jnp.int32, (lats, slots), 0) == (cell >> shift)
            high = current.astype(BF16).astype(F32)
            low = current - high
            weighted = jnp.concatenate(
                [jnp.where(here, high, 0.0).astype(BF16), jnp.where(here, low, 0.0).astype(BF16)], axis=0
            )
            across = one_hot(cell & mask, lons)
            acc = acc + lax.dot_general(
                weighted, across, (((1,), (1,)), ((), ())), preferred_element_type=F32)
        return acc

    acc = lax.fori_loop(0, devices // 4, gathered, jnp.zeros((2 * lats, lons), F32))
    source = acc[:lats] + acc[lats:]

    weight = 4.0 + cond_ref[...]
    row = lax.broadcasted_iota(jnp.int32, (lats, lons), 0)
    potential = jnp.zeros_like(source)
    residual = source
    direction = source
    now = total(residual * residual)
    for _ in range(ITERS):
        south = jnp.where(row == 0, 0.0, pltpu.roll(direction, 1, 0))
        north = jnp.where(row == lats - 1, 0.0, pltpu.roll(direction, lats - 1, 0))
        beside = south + north + pltpu.roll(direction, 1, 1) + pltpu.roll(direction, lons - 1, 1)
        image = weight * direction - beside
        alpha = now / total(direction * image)
        potential = potential + alpha * direction
        residual = residual - alpha * image
        new = total(residual * residual)
        direction = residual + (new / now) * direction
        now = new

    held[...] = potential
    for r in range(share_ref.shape[0]):
        share_ref[r : r + 1, :] = held[pl.ds(first_ref[0] + r, 1), :]
    own = rows_ref[...]
    across = picked(potential, one_hot(jnp.where(own < 0, -1, own & mask), lons))
    here = lax.broadcasted_iota(jnp.int32, across.shape, 0) == (own >> shift)
    added_ref[...] = jnp.sum(jnp.where(here, across, 0.0), axis=0, keepdims=True)


def smem():
    return pl.BlockSpec(memory_space=pltpu.SMEM)


def on_device(state, counts, neighbours, rows, rates, conductance):
    vars_, size, _, _, slots = state.shape
    axes = ("grp", "blk")
    groups, blks = lax.axis_size("grp"), lax.axis_size("blk")
    devices = groups * blks
    blk = lax.axis_index("blk")
    device = lax.axis_index("grp") * blks + blk
    base = jnp.reshape(device * slots, (1,)).astype(jnp.int32)
    half = vars_ // 2
    grid = (half // PAIR,)
    tiles = 2 * size + 4 * (size - 2)
    edge = pl.BlockSpec((PAIR, tiles, size, EDGE), lambda g: (g, 0, 0, 0))
    near = pl.BlockSpec(neighbours.shape, lambda g: (0, 0))
    sums = pl.BlockSpec((1, PAIR, slots), lambda g: (g, 0, 0))
    anywhere = pl.BlockSpec(memory_space=pl.ANY)
    whole = jax.ShapeDtypeStruct(state.shape, F32)
    part = jax.ShapeDtypeStruct((half,) + state.shape[1:], F32)
    edge_shape = jax.ShapeDtypeStruct((half, tiles, size, EDGE), F32)
    sums_shape = jax.ShapeDtypeStruct((half // PAIR, PAIR, slots), F32)
    up = [(d, d + 1) for d in range(devices - 1)]
    down = [(d + 1, d) for d in range(devices - 1)]

    def block(start):
        return pl.BlockSpec((PAIR, size, size, size, slots), lambda g: (g + start // PAIR, 0, 0, 0, 0))

    def exchange(head, tail):
        return lax.ppermute(tail, axes, up), lax.ppermute(head, axes, down)

    def edges(start, *after):
        return pl.pallas_call(
            edges_kernel,
            grid=grid,
            in_specs=[smem(), block(start)] + [anywhere] * len(after),
            out_specs=[edge, edge],
            out_shape=[edge_shape, edge_shape],
            compiler_params=params(),
            cost_estimate=pl.CostEstimate(flops=10**6, bytes_accessed=8 * 10**6, transcendentals=0),
            name="edges",
        )(counts, state, *after)

    def step(kernel, start, u, halo, out_specs, out_shape, extra=(), extra_specs=(), aliases={}):
        return pl.pallas_call(
            functools.partial(kernel, start),
            grid=grid,
            in_specs=[smem(), smem(), smem(), near, edge, edge, block(start if u is state else 0)]
            + list(extra_specs),
            out_specs=out_specs,
            out_shape=out_shape,
            scratch_shapes=[
                pltpu.VMEM((6, slots + 2 * EDGE, slots), BF16),
                pltpu.VMEM((6, PAIR, size, size, slots), F32),
            ],
            input_output_aliases=aliases,
            compiler_params=params(),
            cost_estimate=pl.CostEstimate(flops=5 * 10**9, bytes_accessed=30 * 10**6, transcendentals=0),
            name="step",
        )(base, counts, rates, neighbours, *halo, u, *extra)

    head_b, tail_b = edges(half)
    halo_b = exchange(head_b, tail_b)
    head_a, tail_a = edges(0, head_b)
    head_a, tail_a, *halo_b = lax.optimization_barrier((head_a, tail_a, *halo_b))
    halo_a = exchange(head_a, tail_a)
    outs = [block(0), edge, edge]
    shapes = [part, edge_shape, edge_shape]
    u_b, head_b, tail_b = step(edge_step_kernel, half, state, halo_b, outs, shapes)
    halo_b = exchange(head_b, tail_b)
    u_a, head_a, tail_a = step(edge_step_kernel, 0, state, halo_a, outs, shapes, (head_b,), (anywhere,))
    halo_a = exchange(head_a, tail_a)
    u, faces = step(
        sum_step_kernel, half, u_b, halo_b, [block(half), sums], [whole, sums_shape], (head_a,), (anywhere,))

    lat_rows, lons = conductance.shape
    lats = lat_rows * blks
    own_rows = rows.reshape(1, slots)
    parts, conduct = pl.pallas_call(
        functools.partial(spread_kernel, groups, blks),
        in_specs=[pl.BlockSpec(memory_space=pltpu.VMEM)] * 3,
        out_specs=[pl.BlockSpec(memory_space=pltpu.VMEM)] * 2,
        out_shape=[jax.ShapeDtypeStruct((devices, 2, slots), F32), jax.ShapeDtypeStruct((lats, lons), F32)],
        scratch_shapes=[
            pltpu.VMEM((2, slots), F32),
            pltpu.VMEM((devices, 2, slots), F32),
            pltpu.VMEM((blks, lat_rows, lons), F32),
            pltpu.SemaphoreType.DMA((devices,)),
            pltpu.SemaphoreType.DMA((devices,)),
            pltpu.SemaphoreType.DMA((blks,)),
            pltpu.SemaphoreType.DMA((blks,)),
        ],
        compiler_params=pltpu.CompilerParams(
            vmem_limit_bytes=VMEM_LIMIT, collective_id=0, has_side_effects=True),
        name="spread",
    )(own_rows, faces.reshape(half, slots), conductance)

    first = jnp.reshape(blk * lat_rows, (1,)).astype(jnp.int32)

    def full(*shape):
        return pl.BlockSpec(shape, lambda g: (0,) * len(shape))

    added, share = pl.pallas_call(
        functools.partial(grid_kernel, lons.bit_length() - 1),
        grid=(1,),
        in_specs=[smem(), full(devices, 2, slots), full(lats, lons), full(1, slots)],
        out_specs=[full(1, slots), full(lat_rows, lons)],
        out_shape=[jax.ShapeDtypeStruct((1, slots), F32), jax.ShapeDtypeStruct(conductance.shape, F32)],
        scratch_shapes=[pltpu.VMEM((lats, lons), F32)],
        compiler_params=params(),
        cost_estimate=pl.CostEstimate(flops=5 * 10**9, bytes_accessed=10**6, transcendentals=0),
        name="ionosphere",
    )(first, parts, conduct, own_rows)
    u = step(last_step_kernel, 0, u_a, halo_a, block(0), whole, (added, u), (full(1, slots), anywhere), {8: 0})
    return (u, share)


def solution(mesh):
    placed = (
        P(None, None, None, None, ("grp", "blk")),
        P(("grp", "blk")),
        P(None, ("grp", "blk")),
        P(("grp", "blk")),
        P(),
        P("blk", None),
    )
    return jax.shard_map(
        on_device,
        mesh=mesh,
        in_specs=placed,
        out_specs=(P(None, None, None, None, ("grp", "blk")), P("blk", None)),
        check_vma=False,
    )
```
